32 devices in a mesh: fsdp: 32 (over z, y, x, core).
Axes of the slice: x: 2, y: 2, z: 4, core: 2. Of those that a mesh axis runs over, the one named last changes fastest.
Arguments:
- src_tokens: bfloat16 [32768, 512], P('fsdp'), may hold values from -6 to 6
- tgt_tokens: bfloat16 [32768, 512], P('fsdp'), may hold values from -6 to 6
- src_lengths: int32 [32, 16], P('fsdp'), may hold values from 0 to 128, as said below
- tgt_lengths: int32 [32, 16], P('fsdp'), may hold values from 0 to 128, as said below
- enc_weights: bfloat16 [3147776], P('fsdp'), may hold values from -2 to 2
- dec_weights: bfloat16 [4197376], P('fsdp'), may hold values from -2 to 2
- cotangent: bfloat16 [32768, 512], P('fsdp'), may hold values from -6 to 6, as said below
Outputs:
- decoder_out: bfloat16 [32768, 512], P('fsdp')
- src_grad: float32 [32768, 512], P('fsdp')
- tgt_grad: float32 [32768, 512], P('fsdp')
- enc_grad: float32 [3147776], P('fsdp')
- dec_grad: float32 [4197376], P('fsdp')
The draws below stay inside these ranges and needn't reach their ends.
Inputs may be any that keep to these rules, and one draw needn't show every extreme that they name: `src_lengths`: in each row the sentences fill the first slots and later slots hold 0; a row's lengths sum to at most 1024. A source row and the target row of the same index hold the same number c of sentences, 8 to 16, each of 1024 // c minus at most a quarter of that tokens. Some row holds 16 sentences and some sentence has 128 tokens. `tgt_lengths`: as for src_lengths, with the same count of sentences in each row. `cotangent`: zero at every slot of a target row at or past the sum of that row's tgt_lengths.
All inputs are finite; a program needn't handle non-finite values.
Results may differ from the reference program's by a relative error of at most 0.017.
Values may be sent and summed in bfloat16 or wider, within the bound.
No kernel may reach another device: no remote copies, remote signals or barrier semaphores. Data moves between devices by JAX's collectives and lax.ppermute only.
A program may use at most 384 MiB of HBM per device.

```python
import math
import jax
import jax.numpy as jnp
from jax import lax

D = 512
HEADS = 8
HEAD_DIM = 64
FF = 2048
ROW = 1024
SENTS = 16
BATCH_ROWS = 32
TOKENS = 32768


def sentence_counts(key):
    counts = jax.random.randint(jax.random.fold_in(key, 101), (BATCH_ROWS,), SENTS // 2, SENTS + 1)
    full_row = jax.random.randint(jax.random.fold_in(key, 102), (), 0, BATCH_ROWS)
    offset = jax.random.randint(jax.random.fold_in(key, 103), (), 0, BATCH_ROWS - 1)
    half_row = (full_row + 1 + offset) % BATCH_ROWS
    places = jnp.arange(BATCH_ROWS, dtype=jnp.int32)
    counts = jnp.where(places == full_row, SENTS, jnp.where(places == half_row, SENTS // 2, counts))
    return (counts.astype(jnp.int32), half_row)


def sentence_lengths(key, counts, half_row):
    nominal = (ROW // jnp.maximum(counts, 1))[:, None]
    raw_cut = jax.random.randint(key, (BATCH_ROWS, SENTS), 0, 1048576)
    cut = raw_cut % (nominal // 4 + 1)
    row_index = jnp.arange(BATCH_ROWS, dtype=jnp.int32)[:, None]
    slot_index = jnp.arange(SENTS, dtype=jnp.int32)[None, :]
    cut = jnp.where((row_index == half_row) & (slot_index == 0), 0, cut)
    lengths = nominal - cut
    return jnp.where(slot_index < counts[:, None], lengths, 0).astype(jnp.int32)


def target_lengths(key):
    counts, half_row = sentence_counts(key)
    return sentence_lengths(jax.random.fold_in(key, 2), counts, half_row)


def draw_src_lengths(key, part):
    counts, half_row = sentence_counts(key)
    key = jax.random.fold_in(key, 1)
    return sentence_lengths(key, counts, half_row)


def draw_tgt_lengths(key, part):
    return target_lengths(key)


def draw_cotangent(key, part):
    lengths = target_lengths(key)
    key = jax.random.fold_in(key, 5)
    values = jnp.clip(jax.random.normal(key, (BATCH_ROWS, ROW, D), jnp.float32), -6.0, 6.0)
    totals = jnp.sum(lengths, axis=1)
    places = jnp.arange(ROW, dtype=jnp.int32)
    live = (places[None, :] < totals[:, None]).astype(jnp.float32)
    return (values * live[:, :, None]).reshape(TOKENS, D).astype(jnp.bfloat16)


def flat_draw(key, pieces):
    blocks = []
    for index, (amount, center, spread) in enumerate(pieces):
        subkey = jax.random.fold_in(key, index)
        normal = jnp.clip(jax.random.normal(jax.random.fold_in(subkey, 1), (amount,), jnp.float32), -4.0, 4.0)
        blocks.append(center + spread * normal)
    return jnp.concatenate(blocks).astype(jnp.bfloat16)


def norm_pieces(count):
    return [(D, 1.0, 0.12), (D, 0.0, 0.3)] * count


def draw_enc_weights(key, part):
    key = jax.random.fold_in(key, 3)
    square = D * D
    pieces = [(square, 0.0, D ** (-0.5))] * 3 + [(square, 0.0, (D // 16) ** (-0.5))]
    pieces = pieces + [(D * FF, 0.0, D ** (-0.5)), (FF * D, 0.0, FF ** (-0.5))] + norm_pieces(2)
    return flat_draw(key, pieces)


def draw_dec_weights(key, part):
    key = jax.random.fold_in(key, 4)
    square = D * D
    attention = [(square, 0.0, D ** (-0.5))] * 3 + [(square, 0.0, (D // 16) ** (-0.5))]
    pieces = attention + attention + [(D * FF, 0.0, D ** (-0.5)), (FF * D, 0.0, FF ** (-0.5))] + norm_pieces(3)
    return flat_draw(key, pieces)


def level_of(key, extent, split, smallest, high):
    factor_of, own = 1.0, jax.random.fold_in(key, 6)
    for axis_at, shards_of in split:
        steps = jnp.exp(jax.random.uniform(jax.random.fold_in(own, axis_at), (shards_of,), jnp.float32, smallest / len(split), high / len(split)))
        factor_of = factor_of * jnp.repeat(steps, extent[axis_at] // shards_of).reshape([-1 if axis == axis_at else 1 for axis in range(len(extent))])
    return factor_of


def scatter_about(key, dims, scale, bound, cuts=(), held_as=jnp.bfloat16):
    loudness = level_of(key, dims, cuts, -0.22, 0.18) if cuts else 1.0
    array = jax.random.normal(key, dims, jnp.float32) * scale * loudness
    return jnp.minimum(jnp.maximum(array, -bound), bound).astype(held_as)


def setup_inputs(seed: int = 0) -> dict:
    arg_keys = jax.random.split(jax.random.key(seed), 8)
    return {
        "src_tokens": scatter_about(arg_keys[0], (TOKENS, D), 1.0, 6.0, ((0, 32),)),
        "tgt_tokens": scatter_about(arg_keys[1], (TOKENS, D), 1.0, 6.0, ((0, 32),)),
        "src_lengths": draw_src_lengths(jax.random.fold_in(arg_keys[7], 71), 0),
        "tgt_lengths": draw_tgt_lengths(jax.random.fold_in(arg_keys[7], 71), 0),
        "enc_weights": draw_enc_weights(jax.random.fold_in(arg_keys[7], 71), 0),
        "dec_weights": draw_dec_weights(jax.random.fold_in(arg_keys[7], 71), 0),
        "cotangent": draw_cotangent(jax.random.fold_in(arg_keys[7], 71), 0),
    }


EPSILON = 1e-05
MASKED = -1e+30
HIGHEST_PRECISION = lax.Precision.HIGHEST

@jax.custom_vjp
def low(v):
    return lax.optimization_barrier(v.astype(jnp.bfloat16)).astype(jnp.float32)

@jax.custom_vjp
def low_back(v):
    return v

def low_keep(v):
    return (low(v), None)

def low_pass(kept, grad):
    return (grad,)

def back_keep(v):
    return (v, None)

def back_low(kept, grad):
    return (low(grad),)
low.defvjp(low_keep, low_pass)
low_back.defvjp(back_keep, back_low)

def encoder_layout():
    return [(D, D)] * 4 + [(D, FF), (FF, D)] + [(D,)] * 4

def decoder_layout():
    return [(D, D)] * 8 + [(D, FF), (FF, D)] + [(D,)] * 6

def unpack(flat, layout):
    pieces = []
    offset = 0
    for extents in layout:
        amount = math.prod(extents)
        pieces.append(flat[offset:offset + amount].reshape(extents))
        offset = offset + amount
    return pieces

def dense(left, right):
    return jnp.dot(left, right, precision=HIGHEST_PRECISION, preferred_element_type=jnp.float32)

def segments(lengths, width):
    ends = jnp.cumsum(lengths)
    places = jnp.arange(width, dtype=jnp.int32)
    return lax.optimization_barrier(jnp.sum((places[:, None] >= ends[None, :]).astype(jnp.int32), axis=1))

def allowed_of(seg_query, seg_keys, causal):
    allowed = seg_query[:, None] == seg_keys[None, :]
    if causal:
        places = jnp.arange(seg_query.shape[0], dtype=jnp.int32)
        allowed = allowed & (places[:, None] >= places[None, :])
    return allowed

def norm(values, gain, bias):
    center = lax.optimization_barrier(jnp.mean(values, axis=-1, keepdims=True))
    shifted = values - center
    spread = lax.optimization_barrier(jnp.mean(shifted * shifted, axis=-1, keepdims=True))
    return shifted * lax.rsqrt(spread + EPSILON) * gain + bias

def gelu_exact(values):
    return jax.nn.gelu(values, approximate=False)

def project(inputs, matrix):
    return low(low_back(dense(inputs, matrix)))

def attend(query, keys, values, allowed):
    heads_query = query.reshape(query.shape[0], HEADS, HEAD_DIM)
    heads_keys = keys.reshape(keys.shape[0], HEADS, HEAD_DIM)
    heads_values = values.reshape(values.shape[0], HEADS, HEAD_DIM)
    products = low_back(jnp.einsum('qhd,khd->hqk', heads_query, heads_keys, precision=HIGHEST_PRECISION))
    scores = jnp.where(allowed[None], products * HEAD_DIM ** (-0.5), MASKED)
    highest = lax.optimization_barrier(jnp.max(scores, axis=-1, keepdims=True))
    weights = jnp.exp(scores - highest)
    shares = weights / lax.optimization_barrier(jnp.sum(weights, axis=-1, keepdims=True))
    mixed = jnp.einsum('hqk,khd->qhd', low(shares), heads_values, precision=HIGHEST_PRECISION)
    return low(low_back(mixed.reshape(query.shape[0], D)))

def forward_row(enc_parts, dec_parts, source, target, src_segment, tgt_segment):
    w_query, w_key, w_value, w_out, w_up, w_down, gain_attn, bias_attn, gain_ffn, bias_ffn = enc_parts
    self_query, self_key, self_value, self_out, cross_query, cross_key, cross_value, cross_out, dec_up, dec_down, gain_self, bias_self, gain_cross, bias_cross, gain_last, bias_last = dec_parts
    enc_attn = attend(project(source, w_query), project(source, w_key), project(source, w_value), allowed_of(src_segment, src_segment, False))
    enc_mid = norm(source + low_back(dense(enc_attn, w_out)), gain_attn, bias_attn)
    enc_pre = low_back(dense(low(enc_mid), w_up))
    enc_hidden = low(gelu_exact(enc_pre))
    encoded = norm(enc_mid + low_back(dense(enc_hidden, w_down)) + source, gain_ffn, bias_ffn)
    dec_attn = attend(project(target, self_query), project(target, self_key), project(target, self_value), allowed_of(tgt_segment, tgt_segment, True))
    first_norm = norm(target + low_back(dense(dec_attn, self_out)), gain_self, bias_self)
    encoded_low = low(encoded)
    attn_cross = attend(project(low(first_norm), cross_query), project(encoded_low, cross_key), project(encoded_low, cross_value), allowed_of(tgt_segment, src_segment, False))
    second_norm = norm(first_norm + low_back(dense(attn_cross, cross_out)), gain_cross, bias_cross)
    dec_pre = low_back(dense(low(second_norm), dec_up))
    dec_hidden = low(gelu_exact(dec_pre))
    return norm(second_norm + low_back(dense(dec_hidden, dec_down)) + target, gain_last, bias_last)

def forward(enc_flat, dec_flat, sources, targets, src_segments, tgt_segments):
    enc_parts = unpack(enc_flat, encoder_layout())
    dec_parts = unpack(dec_flat, decoder_layout())

    def step(carry, items):
        return (carry, forward_row(enc_parts, dec_parts, items[0], items[1], items[2], items[3]))
    carry, finals = lax.scan(jax.checkpoint(step), jnp.zeros((), jnp.float32), (sources, targets, src_segments, tgt_segments))
    return finals

def reference(src_tokens, tgt_tokens, src_lengths, tgt_lengths, enc_weights, dec_weights, cotangent):
    sources = src_tokens.astype(jnp.float32).reshape(BATCH_ROWS, ROW, D)
    targets = tgt_tokens.astype(jnp.float32).reshape(BATCH_ROWS, ROW, D)

    def row_segments(lengths):
        return segments(lengths, ROW)
    src_segments = jax.vmap(row_segments)(src_lengths)
    tgt_segments = jax.vmap(row_segments)(tgt_lengths)

    def run(enc_flat, dec_flat, sources_in, targets_in):
        return forward(enc_flat, dec_flat, sources_in, targets_in, src_segments, tgt_segments)
    finals, pullback = jax.vjp(run, enc_weights.astype(jnp.float32), dec_weights.astype(jnp.float32), sources, targets)
    enc_grad, dec_grad, source_grad, target_grad = pullback(cotangent.astype(jnp.float32).reshape(BATCH_ROWS, ROW, D))
    return (finals.reshape(TOKENS, D).astype(jnp.bfloat16), source_grad.reshape(TOKENS, D), target_grad.reshape(TOKENS, D), enc_grad, dec_grad)
```

```python
import functools
import math

import jax
import jax.numpy as jnp
from jax import lax
from jax.experimental import pallas as pl
from jax.experimental.pallas import tpu as pltpu
from jax.sharding import PartitionSpec as P

D=512; TILE=128; SENTS=16; LOWEST=-1e30
NT=(((1,),(1,)),((),())); TN=(((0,),(0,)),((),()))
BF=jnp.bfloat16; F32=jnp.float32

def aligned(at):
    return at if isinstance(at,int) else pl.multiple_of(at,TILE)

def ends_of(ref):
    ends=[]; total=ref[0,0]
    ends.append(total)
    for j in range(1,SENTS):
        total=total+ref[0,j]; ends.append(total)
    return ends

def seg_iota(ends, shape, dim, base=0):
    place=lax.broadcasted_iota(jnp.int32, shape, dim)+base
    seg=jnp.zeros(shape,jnp.int32)
    for e in ends: seg=seg+(place>=e).astype(jnp.int32)
    return seg

def start_of(pos, ends_q, ends_k):
    at=jnp.int32(0)
    for eq,ek in zip(ends_q,ends_k): at=jnp.where(pos>=eq, ek, at)
    return at

def half_lanes(rows):
    return lax.broadcasted_iota(jnp.int32,(rows,TILE),1)<TILE//2

def two_heads(block, low):
    zero=jnp.zeros_like(block)
    return jnp.concatenate([jnp.where(low,block,zero),jnp.where(low,zero,block)],axis=0)

def window_start(kind, tile, blocks, ends_q, ends_k, width):
    if kind=="cross":
        first=start_of(tile*TILE, ends_q, ends_k)//TILE
    else:
        first=tile-1
    return pl.multiple_of(jnp.clip(first,0,blocks-width//TILE)*TILE,TILE)

WIDTH={"full":384,"causal":256,"cross":512}

VM=pl.BlockSpec(memory_space=pltpu.VMEM); SM=pl.BlockSpec(memory_space=pltpu.SMEM)
FF = 2048
EPSILON = 1e-05

def dot(a, b, dims=(((1,), (0,)), ((), ()))):
    return lax.dot_general(a, b, dims, preferred_element_type=F32)


def row_tile(i, size):
    return pl.ds(pl.multiple_of(i * size, size), size)


class Moves:
    def __init__(self, sems):
        self.sems, self.used, self.coming, self.going = sems, 0, [], []

    def copy(self, source, target):
        made = pltpu.make_async_copy(source, target, self.sems.at[self.used])
        self.used += 1
        made.start()
        return made

    def fetch(self, source, target, tile=None):
        self.coming.append((target, tile, self.copy(source, target if tile is None else target.at[rows_of(tile)])))

    def ready(self, *refs, tile=None):
        left = []
        for entry in self.coming:
            if any(entry[0] is ref for ref in refs) and (tile is None or entry[1] in (None, tile)):
                entry[2].wait()
            else:
                left.append(entry)
        self.coming = left

    def ready_all(self):
        for entry in self.coming:
            entry[2].wait()
        self.coming = []

    def send(self, source, target):
        self.going.append(self.copy(source, target))

    def finish(self):
        self.ready_all()
        for made in self.going:
            made.wait()


ROWS = 256


def rows_of(tile):
    return slice(tile * ROWS, (tile + 1) * ROWS)


def call(body, scalars, ins, outs, raw_outs, scratch, micros, raw_ins=(), alias=False, tiled=0):
    ins = [a if isinstance(a, tuple) else (a, 0, a.shape[0]) for a in ins]
    tall = [(count, *a.shape[1:]) for a, _, count in ins]
    tiles = tall[0][0] // ROWS if tiled else 1

    def kernel(*refs):
        refs = list(refs)

        def cut(count):
            taken = refs[:count]
            del refs[:count]
            return taken

        words, sources, raw_in, targets, raw = (
            cut(len(scalars)), cut(len(ins)), cut(len(raw_ins)), cut(len(outs)), cut(len(raw_outs))
        )
        in_refs, out_refs, own = cut(len(ins)), cut(len(outs)), cut(len(scratch))
        moves = Moves(refs[0])
        pairs = list(zip(sources, in_refs, ins))
        for tile in range(tiles):
            for source, target, _ in pairs[:tiled]:
                moves.fetch(source.at[rows_of(tile)], target, tile)
            if tile == 0:
                for source, target, (_, first, count) in pairs[tiled:]:
                    moves.fetch(source.at[pl.ds(first, count)], target)
        place = {id(ref): target for ref, target in zip(out_refs, targets)}

        def emit(*done, tile=None):
            for ref in done:
                part = (lambda r: r) if tile is None else (lambda r: r.at[rows_of(tile)])
                moves.send(part(ref), part(place[id(ref)]))

        body(moves, emit, words, in_refs, raw_in, out_refs, raw, own)
        moves.finish()

    anywhere = pl.BlockSpec(memory_space=pl.ANY)
    held = [*((s, a.dtype) for s, (a, _, _) in zip(tall, ins)), *outs]
    room = sum(math.prod(s) * jnp.dtype(d).itemsize for s, d in held)
    room += sum(math.prod(s.shape) * jnp.dtype(s.dtype).itemsize for s in scratch)
    return pl.pallas_call(
        kernel,
        out_shape=tuple(jax.ShapeDtypeStruct(s, d) for s, d in (*outs, *raw_outs)),
        in_specs=[SM] * len(scalars) + [anywhere] * (len(ins) + len(raw_ins)),
        out_specs=(anywhere,) * (len(outs) + len(raw_outs)),
        scratch_shapes=[
            *(pltpu.VMEM(s, d) for s, d in held),
            *scratch,
            pltpu.SemaphoreType.DMA((len(ins) + tiled * (tiles - 1) + len(outs) * tiles + 8,)),
        ],
        input_output_aliases={len(scalars) + len(ins): len(outs)} if alias else {},
        cost_estimate=pl.CostEstimate(flops=int(micros * 1e10), bytes_accessed=2**20, transcendentals=0),
        compiler_params=pltpu.CompilerParams(vmem_limit_bytes=max(room + 8 * 2**20, 56 * 2**20)),
    )(*scalars, *(a for a, _, _ in ins), *raw_ins)


class Plain:
    def __init__(self, base, ref):
        self.base, self.ref = base, ref

    def put(self, first, value):
        if first - self.base < self.ref.shape[0]:
            self.ref[first - self.base : first - self.base + value.shape[0], :] = value


class Laid:
    def __init__(self, rows, base, ref):
        self.rows, self.base, self.ref = rows, base, ref

    def put(self, first, value):
        last = first + value.shape[0]
        for owner in range(first // self.rows, (last - 1) // self.rows + 1):
            low, high = max(first, owner * self.rows), min(last, (owner + 1) * self.rows)
            self.store(owner, low - owner * self.rows, value[low - first : high - first])
            if low == owner * self.rows:
                self.store(owner - 1, self.rows, value[low - first : low - first + 16])

    def store(self, owner, at, value):
        if 0 <= owner - self.base < self.ref.shape[0]:
            self.ref[owner - self.base, at : at + value.shape[0], :] = value


class Owned(Laid):
    def __init__(self, rows, base, kept, sent):
        self.rows, self.base, self.kept, self.sent = rows, base, kept, sent
        self.core = lax.axis_index("fsdp") % 2

    def store(self, owner, at, value):
        pair = (owner - self.base) // 2
        if not 0 <= pair < self.kept.shape[0]:
            return

        @pl.when(self.core == owner % 2)
        def _():
            self.kept[pair, at : at + value.shape[0], :] = value

        @pl.when(self.core != owner % 2)
        def _():
            self.sent[pair, at : at + value.shape[0], :] = value


def sinks_of(plan, refs):
    if plan[0] == "plain":
        return [Plain(plan[1], refs[0])]
    if plan[0] == "laid":
        return [Laid(plan[1], plan[2], refs[0])]
    return [Owned(plan[1], base, refs[2 * i], refs[2 * i + 1]) for i, (base, _) in enumerate(plan[2])]


def sink_shapes(plan):
    if plan[0] == "plain":
        return [((plan[2], D), BF)]
    if plan[0] == "laid":
        return [((plan[3], plan[1] + 16, D), BF)]
    return [((owners // 2, plan[1] + 16, D), BF) for _, owners in plan[2] for _ in range(2)]


def send_blocks(moves, sink, whole, seal=None):
    count, base, rows = sink.ref.shape[0], sink.base, sink.rows
    moves.send(sink.ref.at[pl.ds(0, count - 1)], whole.at[pl.ds(base, count - 1)])
    moves.send(sink.ref.at[count - 1, pl.ds(0, rows)], whole.at[base + count - 1, pl.ds(0, rows)])
    if base:
        moves.send(sink.ref.at[0, pl.ds(0, 16)], whole.at[base - 1, pl.ds(rows, 16)])
    if seal is not None:
        moves.send(seal, whole.at[whole.shape[0] - 1, pl.ds(rows, 16)])


def laid_shape(plan, n):
    return ((n, plan[1] + 16, D), BF)


def put_all(sinks, first, value):
    for sink in sinks:
        sink.put(first, value)


def matrix(ref, first, rows):
    if len(ref.shape) == 2:
        return ref[first : first + rows, :]
    each = ref.shape[1] - 16
    return ref[first // each : (first + rows) // each, :each, :].reshape(rows, D)


def part_of(w, first, rows):
    each = 1 if len(w.shape) == 2 else w.shape[1] - 16
    return w, first // each, rows // each


def normed(values, gain, bias):
    center = jnp.mean(values, axis=1, keepdims=True)
    shifted = values - center
    spread = jnp.mean(shifted * shifted, axis=1, keepdims=True)
    return shifted * lax.rsqrt(spread + EPSILON) * gain + bias


def norm_back(values, gain, upstream):
    center = jnp.mean(values, axis=1, keepdims=True)
    shifted = values - center
    r = lax.rsqrt(jnp.mean(shifted * shifted, axis=1, keepdims=True) + EPSILON)
    hat = shifted * r
    scaled = upstream * gain
    inner = jnp.mean(scaled * hat, axis=1, keepdims=True)
    grad = r * (scaled - jnp.mean(scaled, axis=1, keepdims=True) - hat * inner)
    return grad, jnp.sum(upstream * hat, axis=0, keepdims=True), jnp.sum(upstream, axis=0, keepdims=True)


def gelu_both(u):
    bell = jnp.exp(u * u * -0.5)
    t = 1.0 / (1.0 + jnp.abs(u) * (0.3275911 * 0.7071067811865476))
    poly = 0.5 * 1.061405429 * t - 0.5 * 1.453152027
    for c in (1.421413741, -0.284496736, 0.254829592):
        poly = poly * t + 0.5 * c
    tail = poly * t * bell
    cdf = jnp.where(u >= 0, 1.0 - tail, tail)
    return u * cdf, cdf + u * bell * 0.3989422804014327


def interleave(size):
    out = lax.broadcasted_iota(jnp.int32, (size, size), 0)
    come = lax.broadcasted_iota(jnp.int32, (size, size), 1)
    quarter = size // 4
    return jnp.where((out % quarter) * 4 + out // quarter == come, 1.0, 0.0).astype(BF)


def ffn_fwd_body(at, moves, emit, words, ins, raw_in, outs, raw, own):
    a_ref, res_ref, w_ref, vec_ref = ins
    h_ref, gp_ref, v_ref, low_ref, wup_ref = outs
    tokens = a_ref.shape[0]
    order = interleave(256)
    moves.ready(w_ref)
    for g in range(FF // 256):
        block = dot(order, matrix(w_ref, g * 256, 256)).astype(BF)
        for k in range(4):
            wup_ref[k, g * 64 : (g + 1) * 64, :] = block[k * 64 : (k + 1) * 64]
    emit(wup_ref)
    moves.ready(vec_ref)
    gain, bias = vec_ref[at : at + 1, :], vec_ref[at + 1 : at + 2, :]
    for i in range(tokens // ROWS):
        rows = rows_of(i)
        moves.ready(a_ref, res_ref, tile=i)
        a = a_ref[rows, :]
        low = a.astype(BF)
        total = a + res_ref[rows, :].astype(F32)
        for k in range(4):
            lanes = slice(k * D, (k + 1) * D)
            act, slope = gelu_both(dot(low, wup_ref[k]))
            act = act.astype(BF)
            h_ref[rows, lanes] = act
            gp_ref[rows, lanes] = slope.astype(BF)
            total = total + dot(act, matrix(w_ref, FF + k * D, D))
        v_ref[rows, :] = total
        low_ref[rows, :] = normed(total, gain, bias).astype(BF)
        emit(low_ref, v_ref, h_ref, gp_ref, tile=i)


def ffn_fwd(at, base, a, res, w, vecs):
    t = a.shape[0]
    return call(
        functools.partial(ffn_fwd_body, at),
        (),
        (a, res, part_of(w, base, 2 * FF), vecs),
        [((t, FF), BF), ((t, FF), BF), ((t, D), F32), ((t, D), BF), ((4, D, D), BF)],
        [],
        [],
        12,
        tiled=2,
    )


def ffn_bwd_body(at, before, plan, base, seal, count, moves, emit, words, ins, raw_in, outs, raw, own):
    e_ref, v_ref, gp_ref, pre_ref, down_ref, wup_ref, vec_ref, h_ref, low_ref = ins
    sink_refs, (dgb_ref, ds_ref, dp_ref) = outs[:count], outs[count:]
    du_ref, dsl_ref, dk_ref, *more_own = own
    sink_refs = more_own or sink_refs
    sinks = sinks_of(plan, sink_refs)
    tokens = v_ref.shape[0]
    moves.ready(down_ref, wup_ref, vec_ref)
    gain, gain_pre = vec_ref[at : at + 1, :], vec_ref[before : before + 1, :]

    sums = (jnp.zeros((1, D), F32),) * 4
    for i in range(tokens // ROWS):
        rows = rows_of(i)
        moves.ready(e_ref, v_ref, gp_ref, pre_ref, tile=i)
        grad, dg, db = norm_back(v_ref[rows, :], gain, e_ref[rows, :].astype(F32))
        ds_ref[rows, :] = grad
        gl = grad.astype(BF)
        dsl_ref[rows, :] = gl
        for k in range(4):
            lanes = slice(k * D, (k + 1) * D)
            du = (dot(gl, matrix(down_ref, k * D, D), NT) * gp_ref[rows, lanes].astype(F32)).astype(BF)
            du_ref[rows, lanes] = du
            grad = grad + dot(du, wup_ref[k], NT)
        grad, dg_pre, db_pre = norm_back(pre_ref[rows, :], gain_pre, grad)
        dp_ref[rows, :] = grad
        emit(dp_ref, ds_ref, tile=i)
        sums = tuple(c + d for c, d in zip(sums, (dg_pre, db_pre, dg, db)))

    vectors = jnp.concatenate([*sums, jnp.zeros((12, D), F32)], axis=0)
    dgb_ref[...] = vectors
    if seal is not None:
        put_all(sinks, seal, vectors.astype(BF))
    emit(dgb_ref)
    moves.ready(h_ref, low_ref)
    for k in range(8):
        piece = dot(h_ref[:, k * 256 : (k + 1) * 256], dsl_ref[...], TN).astype(BF)
        put_all(sinks, base + FF + k * 256, piece)
    for k in range(4):
        for half in range(2):
            lanes = slice(half * 256, (half + 1) * 256)
            dk_ref[k, lanes, :] = dot(low_ref[:, lanes], du_ref[:, k * D : (k + 1) * D], TN).astype(BF)
    order = interleave(256)
    for g in range(FF // 256):
        block = jnp.concatenate([dk_ref[k, g * 64 : (g + 1) * 64, :] for k in range(4)], axis=0)
        put_all(sinks, base + g * 256, dot(order, block, TN).astype(BF))
    if raw:
        send_blocks(moves, sinks[0], raw[0])
    else:
        emit(*sink_refs)


def ffn_bwd(at, before, plan, base, e, v, h, gp, low, pre, wup, w, vecs, seal=None):
    t = v.shape[0]
    shapes, raw = ([], [laid_shape(plan, w.shape[0])]) if plan[0] == "laid" else (sink_shapes(plan), [])
    outs = call(
        functools.partial(ffn_bwd_body, at, before, plan, base, seal, len(shapes)),
        (),
        (e, v, gp, pre, part_of(w, base + FF, FF), wup, vecs, h, low),
        [*shapes, ((16, D), F32), ((t, D), F32), ((t, D), F32)],
        raw,
        [pltpu.VMEM((t, FF), BF), pltpu.VMEM((t, D), BF), pltpu.VMEM((4, D, D), BF)]
        + [pltpu.VMEM(*s) for s in (sink_shapes(plan) if raw else [])],
        13,
        tiled=4,
    )
    if raw:
        return outs[3:], *outs[:3]
    return outs[: len(shapes)], *outs[len(shapes) :]


def attn_fwd_body(kind, at, moves, emit, words, ins, raw_in, outs, raw, own):
    lq_ref, lk_ref = words
    xq_ref, xk_ref, w_ref, vec_ref = ins if kind == "cross" else (ins[0], *ins)
    q_ref, k_ref, v_ref, o_ref, pre_ref, out_ref, low_ref = outs
    (segk_ref,) = own
    tokens = q_ref.shape[0]
    blocks, width = tokens // TILE, WIDTH[kind]
    ends_q, ends_k = ends_of(lq_ref), ends_of(lk_ref)
    segk_ref[...] = seg_iota(ends_k, (8, tokens), 1)
    low = half_lanes(TILE)
    moves.ready(w_ref)
    for i in range(tokens // ROWS):
        rows = rows_of(i)
        moves.ready(xq_ref, xk_ref, tile=i)
        xq, xk = xq_ref[rows, :].astype(BF), xk_ref[rows, :].astype(BF)
        q_ref[rows, :] = dot(xq, matrix(w_ref, 0, D)).astype(BF)
        k_ref[rows, :] = dot(xk, matrix(w_ref, D, D)).astype(BF)
        v_ref[rows, :] = dot(xk, matrix(w_ref, 2 * D, D)).astype(BF)
    emit(q_ref, k_ref, v_ref)

    def one(tile, start, width):
        rows = row_tile(tile, TILE)
        seg_q = seg_iota(ends_q, (TILE, TILE), 0, tile * TILE)
        biases = []
        for b in range(width // TILE):
            ok = seg_q == segk_ref[0:1, pl.ds(aligned(start + b * TILE), TILE)]
            if kind == "causal":
                gap = lax.broadcasted_iota(jnp.int32, (TILE, TILE), 0) - lax.broadcasted_iota(jnp.int32, (TILE, TILE), 1)
                ok = ok & (gap >= start + b * TILE - tile * TILE)
            biases.append(jnp.where(ok, 0.0, LOWEST))
        bias_q = jnp.concatenate(biases, axis=1)
        bias_q = jnp.concatenate([bias_q, bias_q], axis=0)
        outs = []
        for p in range(D // TILE):
            lanes = slice(p * TILE, (p + 1) * TILE)
            q2 = two_heads(q_ref[rows, lanes].astype(F32) * 0.125, low).astype(BF)
            s = dot(q2, k_ref[pl.ds(start, width), lanes], NT) + bias_q
            e = jnp.exp(s - jnp.max(s, axis=1, keepdims=True)).astype(BF)
            vx = jnp.concatenate([v_ref[pl.ds(start, width), lanes], jnp.ones((width, TILE), BF)], axis=1)
            o2 = dot(e, vx)
            o2 = o2[:, :TILE] / o2[:, TILE:]
            outs.append(jnp.where(low, o2[:TILE], o2[TILE:]))
        return jnp.concatenate(outs, axis=1)

    def step(tile, _):
        rows = row_tile(tile, TILE)
        start = window_start(kind, tile, blocks, ends_q, ends_k, width)
        o_ref[rows, :] = one(tile, start, width).astype(BF)
        tail = (blocks - 3) * TILE
        if kind == "cross":
            more = ends_q[-1] < (tile + 1) * TILE
        elif kind == "full":
            more = (tile == blocks - 3) & (ends_q[-1] < tail + TILE)
        else:
            more = (tile == blocks - 1) & (ends_q[-1] < tail + TILE)

        @pl.when(more)
        def _():
            o = one(tile, tail, 3 * TILE)
            if kind == "cross":
                mean = jnp.sum(v_ref[...].astype(F32), axis=0, keepdims=True) * (1.0 / tokens)
                o = jnp.where(ends_k[-1] >= tokens, jnp.broadcast_to(mean, o.shape), o)
            pad = lax.broadcasted_iota(jnp.int32, (TILE, D), 0) + tile * TILE >= ends_q[-1]
            o_ref[rows, :] = jnp.where(pad, o, o_ref[rows, :].astype(F32)).astype(BF)

        return 0

    lax.fori_loop(0, blocks, step, 0)
    emit(o_ref)
    moves.ready(vec_ref)
    gain, bias = vec_ref[at : at + 1, :], vec_ref[at + 1 : at + 2, :]

    for i in range(tokens // ROWS):
        rows = rows_of(i)
        total = xq_ref[rows, :].astype(F32) + dot(o_ref[rows, :], matrix(w_ref, 3 * D, D))
        pre_ref[rows, :] = total
        out = normed(total, gain, bias)
        out_ref[rows, :] = out
        low_ref[rows, :] = out.astype(BF)
        emit(out_ref, low_ref, pre_ref, tile=i)


def attn_fwd(kind, at, base, lq, lk, xq, xk, w, vecs):
    t = xq.shape[0]
    low, full = ((t, D), BF), ((t, D), F32)
    return call(
        functools.partial(attn_fwd_body, kind, at),
        (lq, lk),
        ((xq, xk) if kind == "cross" else (xq,)) + (part_of(w, base, 4 * D), vecs),
        [low, low, low, low, full, full, low],
        [],
        [pltpu.VMEM((8, t), jnp.int32)],
        12,
        tiled=2 if kind == "cross" else 1,
    )


def attn_bwd_body(kind, before, plan, base, seal, count, moves, emit, words, ins, raw_in, outs, raw, own):
    cross = kind == "cross"
    lq_ref, lk_ref = words
    if cross:
        ds_ref, w_ref, q_ref, k_ref, v_ref, vec_ref, more_ref, xq_ref, xk_ref, o_ref, dgb_in_ref = ins
        sink_refs, (dgb_ref, dx_ref, dxk_ref) = outs[:count], outs[count:]
    else:
        ds_ref, w_ref, q_ref, k_ref, v_ref, vec_ref, more_ref, xq_ref, o_ref, dgb_in_ref = ins
        xk_ref, dxk_ref = xq_ref, None
        sink_refs, (dx_ref,) = outs[:count], outs[count:]
    segq_ref, segk_ref, dk_acc, dv_acc, dsl_ref, g_ref, dq_ref, dk_ref, dv_ref, *more_own = own
    seal_ref = None
    if raw:
        *sink_refs, seal_ref = more_own
    sinks = sinks_of(plan, sink_refs)
    if not raw:
        for source, target in zip(raw_in, sink_refs):
            pairs = source.shape[0]
            moves.fetch(source, target.at[pl.ds(target.shape[0] - pairs, pairs)])
    tokens = q_ref.shape[0]
    blocks, width = tokens // TILE, WIDTH[kind]
    ends_q, ends_k = ends_of(lq_ref), ends_of(lk_ref)
    segq_ref[...] = seg_iota(ends_q, (8, tokens), 1)
    segk_ref[...] = seg_iota(ends_k, (tokens, TILE), 0)
    dk_acc[...] = jnp.zeros_like(dk_acc)
    dv_acc[...] = jnp.zeros_like(dv_acc)
    low = half_lanes(TILE)
    moves.ready(w_ref)
    for i in range(tokens // ROWS):
        rows = rows_of(i)
        moves.ready(ds_ref, tile=i)
        gl = ds_ref[rows, :].astype(BF)
        dsl_ref[rows, :] = gl
        g_ref[rows, :] = dot(gl, matrix(w_ref, 3 * D, D), NT).astype(BF)
    moves.ready(q_ref, k_ref, v_ref)

    def step(tile, _):
        rows = row_tile(tile, TILE)
        start = window_start(kind, tile, blocks, ends_q, ends_k, width)
        win = pl.ds(start, width)
        ok = segk_ref[win, :] == segq_ref[0:1, rows]
        if kind == "causal":
            gap = lax.broadcasted_iota(jnp.int32, (width, TILE), 1) - lax.broadcasted_iota(jnp.int32, (width, TILE), 0)
            ok = ok & (gap >= start - tile * TILE)
        bias = jnp.where(ok, 0.0, LOWEST)
        bias = jnp.concatenate([bias, bias], axis=1)
        for p in range(D // TILE):
            lanes = slice(p * TILE, (p + 1) * TILE)
            q2 = two_heads(q_ref[rows, lanes].astype(F32) * 0.125, low).astype(BF)
            g2 = two_heads(g_ref[rows, lanes].astype(F32), low).astype(BF)
            kp, vp = k_ref[win, lanes], v_ref[win, lanes]
            s = dot(kp, q2, NT) + bias
            e = jnp.exp(s - jnp.max(s, axis=0, keepdims=True))
            prob = e * (1.0 / jnp.sum(e, axis=0, keepdims=True))
            t = prob * dot(vp, g2, NT)
            ds = (t - prob * jnp.sum(t, axis=0, keepdims=True)).astype(BF)
            dk_acc[win, lanes] += dot(ds, q2)
            dv_acc[win, lanes] += dot(prob.astype(BF), g2)
            dq = dot(ds, kp, TN)
            dq_ref[rows, lanes] = (jnp.where(low, dq[:TILE], dq[TILE:]) * 0.125).astype(BF)
        return 0

    lax.fori_loop(0, blocks, step, 0)
    moves.ready(vec_ref, more_ref)

    sums = (jnp.zeros((1, D), F32),) * 2
    for i in range(tokens // ROWS):
        rows = rows_of(i)
        dk, dv = dk_acc[rows, :].astype(BF), dv_acc[rows, :].astype(BF)
        dk_ref[rows, :], dv_ref[rows, :] = dk, dv
        from_q = ds_ref[rows, :] + dot(dq_ref[rows, :], matrix(w_ref, 0, D), NT)
        from_k = dot(dk, matrix(w_ref, D, D), NT) + dot(dv, matrix(w_ref, 2 * D, D), NT)
        if not cross:
            dx_ref[rows, :] = more_ref[rows, :] + from_q + from_k
            emit(dx_ref, tile=i)
            continue
        dxk_ref[rows, :] = from_k
        grad, dg, db = norm_back(more_ref[rows, :], vec_ref[before : before + 1, :], from_q)
        dx_ref[rows, :] = grad
        emit(dx_ref, dxk_ref, tile=i)
        sums = sums[0] + dg, sums[1] + db
    moves.ready(dgb_in_ref)
    if cross:
        dgb_ref[...] = jnp.concatenate([*sums, dgb_in_ref[:14, :]], axis=0)
        emit(dgb_ref)
    moves.ready_all()
    for m, (left_ref, right_ref) in enumerate(((xq_ref, dq_ref), (xk_ref, dk_ref), (xk_ref, dv_ref), (o_ref, dsl_ref))):
        for half in range(2):
            piece = dot(left_ref[:, half * 256 : (half + 1) * 256], right_ref[...], TN).astype(BF)
            put_all(sinks, base + m * D + half * 256, piece)
    if not raw:
        emit(*sink_refs)
    elif cross:
        send_blocks(moves, sinks[0], raw[0])
    else:
        seal_ref[...] = dgb_in_ref[...].astype(BF)
        send_blocks(moves, sinks[0], raw[0], seal_ref)


def attn_bwd(kind, before, plan, base, lq, lk, ds, q, k, v, o, xq, xk, w, vecs, more, dgb, taken=()):
    t = xq.shape[0]
    low, full = ((t, D), BF), ((t, D), F32)
    vm = pltpu.VMEM
    shapes, raw = ([], [laid_shape(plan, w.shape[0])]) if plan[0] == "laid" else (sink_shapes(plan), [])
    scratch = [vm((8, t), jnp.int32), vm((t, TILE), jnp.int32), vm(*full), vm(*full)] + [vm(*low)] * 5
    if raw:
        scratch += [*(vm(*s) for s in sink_shapes(plan)), vm((16, D), BF)]
    outs = call(
        functools.partial(attn_bwd_body, kind, before, plan, base, None, len(shapes)),
        (lq, lk),
        (ds, part_of(w, base, 4 * D), q, k, v, vecs, more) + ((xq, xk) if kind == "cross" else (xq,)) + (o, dgb),
        [*shapes] + ([((16, D), F32), full, full] if kind == "cross" else [full]),
        raw,
        scratch,
        26,
        raw_ins=taken,
        alias=bool(raw),
        tiled=1,
    )
    if raw:
        return outs[-1:], *outs[:-1]
    return outs[: len(shapes)], *outs[len(shapes) :]


SIDES = {"z": 4, "y": 2, "x": 2, "core": 2}
STRIDE = {"z": 8, "y": 4, "x": 2, "core": 1}


def place_of(name):
    return lax.axis_index("fsdp") // STRIDE[name] % SIDES[name]


def shifted(block, name, step, n=32):
    side, stride = SIDES[name], STRIDE[name]
    pairs = []
    for device in range(n):
        at = device // stride % side
        pairs.append((device, device + ((at + step) % side - at) * stride))
    return lax.ppermute(block, "fsdp", pairs)


def spread(pieces, order):
    for name in order:
        if len(pieces) > 1:
            pieces = [(jnp.concatenate([p for p, _ in pieces]), sum((l for _, l in pieces), []))]
        held, labels = pieces[0]
        spot = "zyx".index(name)
        for step in range(1, SIDES[name]):
            moved = [tuple(v + step * (i == spot) for i, v in enumerate(label)) for label in labels]
            pieces.append((shifted(held, name, step), moved))
    both = [(p, [l + (0,) for l in labels]) for p, labels in pieces]
    both += [(shifted(p, "core", 1), [l + (1,) for l in labels]) for p, labels in pieces]
    return both


def assemble_kernel(spans, labels, counts, vectors, *refs):
    *pieces, rows_ref, vecs_ref, tails, row_sem, tail_sem = refs
    n, rows = counts
    me = lax.axis_index("fsdp")
    z, y, x, core = me // 8, me // 4 % 2, me // 2 % 2, me % 2
    for piece, (first, last), names in zip(pieces, spans, labels):
        for at, (dz, dy, dx, dc) in enumerate(names):
            owner = (((z + 4 - dz) % 4 * 2 + (y + dy) % 2) * 2 + (x + dx) % 2) * 2 + (core + dc) % 2
            whole = min(last, rows) - first
            if whole:
                pltpu.make_async_copy(
                    piece.at[at, pl.ds(0, whole)], rows_ref.at[owner, pl.ds(first, whole)], row_sem
                ).start()
            if last > rows:
                pltpu.make_async_copy(
                    piece.at[at, pl.ds(whole, last - rows)], tails.at[owner], tail_sem
                ).start()
    pltpu.make_async_copy(rows_ref, rows_ref, row_sem).wait()
    pltpu.make_async_copy(tails, tails, tail_sem).wait()
    spill = lax.broadcasted_iota(jnp.int32, (16, D), 0) < vectors
    for owner in range(1, n):
        tail = jnp.where(spill, tails[owner - 1].astype(F32), 0.0)
        rows_ref[owner, 0:16] = (rows_ref[owner, 0:16].astype(F32) + tail).astype(BF)
    vecs_ref[...] = tails[n - 1].astype(F32)


def assemble(parts, n, rows, vectors):
    pieces, spans, labels = [], [], []
    for first, last, held in parts:
        for piece, names in held:
            pieces.append(piece)
            spans.append((first, last))
            labels.append(names)
    return pl.pallas_call(
        functools.partial(assemble_kernel, spans, labels, (n, rows), vectors),
        out_shape=(jax.ShapeDtypeStruct((n, rows, D), BF), jax.ShapeDtypeStruct((16, D), F32)),
        in_specs=[pl.BlockSpec(memory_space=pl.ANY)] * len(pieces),
        out_specs=(VM, VM),
        scratch_shapes=[pltpu.VMEM((n, 16, D), BF), pltpu.SemaphoreType.DMA, pltpu.SemaphoreType.DMA],
        compiler_params=pltpu.CompilerParams(vmem_limit_bytes=16 * 2**20),
    )(*pieces)


def geometry(local, n, vectors):
    rows = (local * n // D - vectors) // n
    return rows, rows + 16


def own_rows(flat, vectors, n):
    local = flat.shape[0]
    rows, block = geometry(local, n, vectors)
    extra = vectors * D // n
    room = jnp.pad(flat, (vectors * D, block * D - local))
    return lax.dynamic_slice(room, (vectors * D - extra * lax.axis_index("fsdp"),), (block * D,)).reshape(block, D)


def gather_whole(own, vectors, n):
    block = own.shape[0]
    rows = block - 16
    full = lax.all_gather(own, "fsdp", axis=0, tiled=True).reshape(n, block, D)
    spill = jnp.arange(16)[:, None] < vectors
    tails = jnp.where(spill, full[:-1, rows:], 0)
    return full.at[1:, :16].add(tails), full[-1, rows:].astype(F32)


def gather_plain(own, vectors, n):
    full, vecs = gather_whole(own, vectors, n)
    return full[:, : own.shape[0] - 16].reshape(-1, D), vecs


def gather_parts(own, vectors, n):
    rows = own.shape[0] - 16
    full, vecs = assemble(three_ways(own), n, rows, vectors)
    return full.reshape(n * rows, D), vecs


def three_ways(own):
    edges = [0, 48, 128, own.shape[0]]
    return [(a, b, spread([(own[None, a:b], [(0, 0, 0)])], order)) for a, b, order in zip(edges, edges[1:], ("xyz", "yzx", "zxy"))]


def pick(array, at, axis):
    return lax.dynamic_index_in_dim(array, at, axis, keepdims=False)


def total_of(terms):
    return sum(t.astype(F32) for t in terms)


def halve(terms, name, axis):
    at = place_of(name)
    away = total_of([pick(t, 1 - at, axis) for t in terms]).astype(BF)
    return [pick(t, at, axis) for t in terms] + [shifted(away, name, 1)]


def reduce_plane(kept, sent, order):
    kept, come = (a.reshape(-1, 2, 2, *a.shape[1:]) for a in (kept, shifted(sent, "core", 1)))
    terms = [kept, come]
    if order == "both":
        half = kept.shape[-2] // 32 * 16
        one = halve(halve([t[..., :half, :] for t in terms], "x", 2), "y", 1)
        two = halve(halve([t[..., half:, :] for t in terms], "y", 1), "x", 1)
        return [jnp.concatenate([a, b], axis=1) for a, b in zip(one, two)]
    if order == "xy":
        return halve(halve(terms, "x", 2), "y", 1)
    return halve(halve(terms, "y", 1), "x", 1)


def reduce_line(planes, base):
    count = planes[0].shape[0]
    z = place_of("z")
    sums = total_of(planes).astype(BF)
    pieces = []
    for step in (1, 2, 3):
        pairs = []
        for device in range(32):
            goal = (device // 8 + step) % 4
            if base <= goal < base + count:
                pairs.append((device, goal * 8 + device % 8))
        away = pick(sums, jnp.clip((z + step) % 4 - base, 0, count - 1), 0)
        pieces.append(lax.ppermute(away, "fsdp", pairs))
    return total_of([pick(t, jnp.clip(z - base, 0, count - 1), 0) for t in planes] + pieces)


def own_part(own, vectors, local, n):
    return lax.dynamic_slice(own.reshape(-1), (vectors * D // n * lax.axis_index("fsdp"),), (local,))


def scatter_plain(matrices, vectors_sum, n):
    rows = matrices.shape[0] // n
    blocks = matrices.reshape(n, rows, D)
    tails = jnp.concatenate([blocks[1:, :16], vectors_sum[None].astype(BF)], axis=0)
    terms = jnp.concatenate([blocks, tails], axis=1).reshape(-1, D)
    return lax.psum_scatter(terms, "fsdp", scatter_dimension=0, tiled=True).astype(F32)


def on_device(src, tgt, ls, lt, enc_weights, dec_weights, cotangent, n):
    split = n == 32
    e_own, d_own = own_rows(enc_weights, 4, n), own_rows(dec_weights, 6, n)
    e_own, d_own = lax.optimization_barrier((e_own, d_own))
    e_all, ev = (gather_parts if split else gather_plain)(e_own, 4, n)
    d_all, dv = (gather_whole if split else gather_plain)(d_own, 6, n)
    q1, k1, v1, o1, pre1, ax, axl = attn_fwd("full", 0, 0, ls, ls, src, src, e_all, ev)
    hx, gpx, sum2, enc, wup_e = ffn_fwd(2, FF, ax, src, e_all, ev)
    q3, k3, v3, o3, pre3, h1, h1l = attn_fwd("causal", 0, 0, lt, lt, tgt, tgt, d_all, dv)
    q4, k4, v4, o4, pre4, h2, h2l = attn_fwd("cross", 2, FF, lt, ls, h1, enc, d_all, dv)
    hy, gpy, sum5, final, wup_d = ffn_fwd(4, 2 * FF, h2, tgt, d_all, dv)
    if split:
        d_plan = [("laid", 256, 16, 16), ("laid", 256, 8, 8), ("laid", 256, 0, 8)]
        e_plan = [("owned", 192, ((16, 16), (10, 6))), ("owned", 192, ((0, 16),))]
        seal = 3 * FF
    else:
        d_plan = [("plain", 2 * FF, 2 * FF), ("plain", FF, FF), ("plain", 0, FF)]
        e_plan = [("plain", FF, 2 * FF), ("plain", 0, FF)]
        seal = None
    g, dgb, ds5, ds4 = ffn_bwd(4, 2, d_plan[0], 2 * FF, cotangent, sum5, hy, gpy, h2l, pre4, wup_d, d_all, dv)
    g3 = g
    g, dgb, ds3, denc = attn_bwd(
        "cross", 0, d_plan[1], FF, lt, ls, ds4, q4, k4, v4, o4, h1l, enc, d_all, dv, pre3, dgb, g3 if split else ()
    )
    g2 = g
    g, tgt_grad = attn_bwd(
        "causal", 0, d_plan[2], 0, lt, lt, ds3, q3, k3, v3, o3, tgt, tgt, d_all, dv, ds5, dgb, g2 if split else ()
    )
    g1 = g
    f, egb, ds2, ds1 = ffn_bwd(2, 0, e_plan[0], FF, denc, sum2, hx, gpx, axl, pre1, wup_e, e_all, ev, seal)
    if split:
        d_sum = lax.psum_scatter(g1[0].reshape(-1, D), "fsdp", scatter_dimension=0, tiled=True).astype(F32)
        high = reduce_line(reduce_plane(*f[:2], "yx"), 2)
        a, src_grad = attn_bwd(
            "full", 0, e_plan[1], 0, ls, ls, ds1, q1, k1, v1, o1, src, src, e_all, ev, ds2, egb, f[2:]
        )
        low = reduce_line(reduce_plane(*a, "both"), 0)
        e_sum = jnp.where(place_of("z") >= 2, high, low)
    else:
        a, src_grad = attn_bwd("full", 0, e_plan[1], 0, ls, ls, ds1, q1, k1, v1, o1, src, src, e_all, ev, ds2, egb)
        vecs = lax.psum(jnp.concatenate([egb, dgb]), "fsdp")
        d_sum = scatter_plain(jnp.concatenate([g1[0], g2[0], g3[0]]), vecs[16:], n)
        e_sum = scatter_plain(jnp.concatenate([a[0], f[0]]), vecs[:16], n)
    enc_grad = own_part(e_sum, 4, enc_weights.shape[0], n)
    dec_grad = own_part(d_sum, 6, dec_weights.shape[0], n)
    return final, src_grad, tgt_grad, enc_grad, dec_grad


def solution(mesh):
    n = mesh.shape["fsdp"]
    return jax.shard_map(
        functools.partial(on_device, n=n),
        mesh=mesh,
        in_specs=(P("fsdp", None),) * 4 + (P("fsdp"),) * 2 + (P("fsdp", None),),
        out_specs=(P("fsdp", None),) * 3 + (P("fsdp"),) * 2,
        check_vma=False,
    )
```

```python
import functools
import math

import jax
import jax.numpy as jnp
from jax import lax
from jax.experimental import pallas as pl
from jax.experimental.pallas import tpu as pltpu
from jax.sharding import PartitionSpec as P

D=512; TILE=128; SENTS=16; LOWEST=-1e30
NT=(((1,),(1,)),((),())); TN=(((0,),(0,)),((),()))
BF=jnp.bfloat16; F32=jnp.float32

def aligned(at):
    return at if isinstance(at,int) else pl.multiple_of(at,TILE)

def ends_of(ref):
    ends=[]; total=ref[0,0]
    ends.append(total)
    for j in range(1,SENTS):
        total=total+ref[0,j]; ends.append(total)
    return ends

def seg_iota(ends, shape, dim, base=0):
    place=lax.broadcasted_iota(jnp.int32, shape, dim)+base
    seg=jnp.zeros(shape,jnp.int32)
    for e in ends: seg=seg+(place>=e).astype(jnp.int32)
    return seg

def start_of(pos, ends_q, ends_k):
    at=jnp.int32(0)
    for eq,ek in zip(ends_q,ends_k): at=jnp.where(pos>=eq, ek, at)
    return at

def half_lanes(rows):
    return lax.broadcasted_iota(jnp.int32,(rows,TILE),1)<TILE//2

def two_heads(block, low):
    zero=jnp.zeros_like(block)
    return jnp.concatenate([jnp.where(low,block,zero),jnp.where(low,zero,block)],axis=0)

def window_start(kind, tile, blocks, ends_q, ends_k, width):
    if kind=="cross":
        first=start_of(tile*TILE, ends_q, ends_k)//TILE
    else:
        first=tile-1
    return pl.multiple_of(jnp.clip(first,0,blocks-width//TILE)*TILE,TILE)

WIDTH={"full":384,"causal":256,"cross":512}

VM=pl.BlockSpec(memory_space=pltpu.VMEM); SM=pl.BlockSpec(memory_space=pltpu.SMEM)
FF = 2048
EPSILON = 1e-05

def dot(a, b, dims=(((1,), (0,)), ((), ()))):
    return lax.dot_general(a, b, dims, preferred_element_type=F32)


def row_tile(i, size):
    return pl.ds(pl.multiple_of(i * size, size), size)


class Moves:
    def __init__(self, sems):
        self.sems, self.used, self.coming, self.going = sems, 0, [], []

    def copy(self, source, target):
        made = pltpu.make_async_copy(source, target, self.sems.at[self.used])
        self.used += 1
        made.start()
        return made

    def fetch(self, source, target, tile=None):
        self.coming.append((target, tile, self.copy(source, target if tile is None else target.at[rows_of(tile)])))

    def ready(self, *refs, tile=None):
        left = []
        for entry in self.coming:
            if any(entry[0] is ref for ref in refs) and (tile is None or entry[1] in (None, tile)):
                entry[2].wait()
            else:
                left.append(entry)
        self.coming = left

    def ready_all(self):
        for entry in self.coming:
            entry[2].wait()
        self.coming = []

    def send(self, source, target):
        self.going.append(self.copy(source, target))

    def finish(self):
        self.ready_all()
        for made in self.going:
            made.wait()


ROWS = 512


def rows_of(tile):
    return slice(tile * ROWS, (tile + 1) * ROWS)


def call(body, scalars, ins, outs, raw_outs, scratch, micros, raw_ins=(), alias=False, tiled=0):
    ins = [a if isinstance(a, tuple) else (a, 0, a.shape[0]) for a in ins]
    tall = [(count, *a.shape[1:]) for a, _, count in ins]
    tiles = tall[0][0] // ROWS if tiled else 1

    def kernel(*refs):
        refs = list(refs)

        def cut(count):
            taken = refs[:count]
            del refs[:count]
            return taken

        words, sources, raw_in, targets, raw = (
            cut(len(scalars)), cut(len(ins)), cut(len(raw_ins)), cut(len(outs)), cut(len(raw_outs))
        )
        in_refs, out_refs, own = cut(len(ins)), cut(len(outs)), cut(len(scratch))
        moves = Moves(refs[0])
        pairs = list(zip(sources, in_refs, ins))
        for tile in range(tiles):
            for source, target, _ in pairs[:tiled]:
                moves.fetch(source.at[rows_of(tile)], target, tile)
            if tile == 0:
                for source, target, (_, first, count) in pairs[tiled:]:
                    moves.fetch(source.at[pl.ds(first, count)], target)
        place = {id(ref): target for ref, target in zip(out_refs, targets)}

        def emit(*done, tile=None):
            for ref in done:
                part = (lambda r: r) if tile is None else (lambda r: r.at[rows_of(tile)])
                moves.send(part(ref), part(place[id(ref)]))

        body(moves, emit, words, in_refs, raw_in, out_refs, raw, own)
        moves.finish()

    anywhere = pl.BlockSpec(memory_space=pl.ANY)
    held = [*((s, a.dtype) for s, (a, _, _) in zip(tall, ins)), *outs]
    room = sum(math.prod(s) * jnp.dtype(d).itemsize for s, d in held)
    room += sum(math.prod(s.shape) * jnp.dtype(s.dtype).itemsize for s in scratch)
    return pl.pallas_call(
        kernel,
        out_shape=tuple(jax.ShapeDtypeStruct(s, d) for s, d in (*outs, *raw_outs)),
        in_specs=[SM] * len(scalars) + [anywhere] * (len(ins) + len(raw_ins)),
        out_specs=(anywhere,) * (len(outs) + len(raw_outs)),
        scratch_shapes=[
            *(pltpu.VMEM(s, d) for s, d in held),
            *scratch,
            pltpu.SemaphoreType.DMA((len(ins) + tiled * (tiles - 1) + len(outs) * tiles + 8,)),
        ],
        input_output_aliases={len(scalars) + len(ins): len(outs)} if alias else {},
        cost_estimate=pl.CostEstimate(flops=int(micros * 1e10), bytes_accessed=2**20, transcendentals=0),
        compiler_params=pltpu.CompilerParams(vmem_limit_bytes=max(room + 8 * 2**20, 56 * 2**20)),
    )(*scalars, *(a for a, _, _ in ins), *raw_ins)


class Plain:
    def __init__(self, base, ref):
        self.base, self.ref = base, ref

    def put(self, first, value):
        if first - self.base < self.ref.shape[0]:
            self.ref[first - self.base : first - self.base + value.shape[0], :] = value


class Laid:
    def __init__(self, rows, base, ref):
        self.rows, self.base, self.ref = rows, base, ref

    def put(self, first, value):
        last = first + value.shape[0]
        for owner in range(first // self.rows, (last - 1) // self.rows + 1):
            low, high = max(first, owner * self.rows), min(last, (owner + 1) * self.rows)
            self.store(owner, low - owner * self.rows, value[low - first : high - first])
            if low == owner * self.rows:
                self.store(owner - 1, self.rows, value[low - first : low - first + 16])

    def store(self, owner, at, value):
        if 0 <= owner - self.base < self.ref.shape[0]:
            self.ref[owner - self.base, at : at + value.shape[0], :] = value


class Owned(Laid):
    def __init__(self, rows, base, kept, sent):
        self.rows, self.base, self.kept, self.sent = rows, base, kept, sent
        self.core = lax.axis_index("fsdp") % 2

    def store(self, owner, at, value):
        pair = (owner - self.base) // 2
        if not 0 <= pair < self.kept.shape[0]:
            return

        @pl.when(self.core == owner % 2)
        def _():
            self.kept[pair, at : at + value.shape[0], :] = value

        @pl.when(self.core != owner % 2)
        def _():
            self.sent[pair, at : at + value.shape[0], :] = value


def sinks_of(plan, refs):
    if plan[0] == "plain":
        return [Plain(plan[1], refs[0])]
    if plan[0] == "laid":
        return [Laid(plan[1], plan[2], refs[0])]
    return [Owned(plan[1], base, refs[2 * i], refs[2 * i + 1]) for i, (base, _) in enumerate(plan[2])]


def sink_shapes(plan):
    if plan[0] == "plain":
        return [((plan[2], D), BF)]
    if plan[0] == "laid":
        return [((plan[3], plan[1] + 16, D), BF)]
    return [((owners // 2, plan[1] + 16, D), BF) for _, owners in plan[2] for _ in range(2)]


def put_all(sinks, first, value):
    for sink in sinks:
        sink.put(first, value)


def matrix(ref, first, rows):
    if len(ref.shape) == 2:
        return ref[first : first + rows, :]
    each = ref.shape[1] - 16
    return ref[first // each : (first + rows) // each, :each, :].reshape(rows, D)


def part_of(w, first, rows):
    each = 1 if len(w.shape) == 2 else w.shape[1] - 16
    return w, first // each, rows // each


def normed(values, gain, bias):
    center = jnp.mean(values, axis=1, keepdims=True)
    shifted = values - center
    spread = jnp.mean(shifted * shifted, axis=1, keepdims=True)
    return shifted * lax.rsqrt(spread + EPSILON) * gain + bias


def norm_back(values, gain, upstream):
    center = jnp.mean(values, axis=1, keepdims=True)
    shifted = values - center
    r = lax.rsqrt(jnp.mean(shifted * shifted, axis=1, keepdims=True) + EPSILON)
    hat = shifted * r
    scaled = upstream * gain
    inner = jnp.mean(scaled * hat, axis=1, keepdims=True)
    grad = r * (scaled - jnp.mean(scaled, axis=1, keepdims=True) - hat * inner)
    return grad, jnp.sum(upstream * hat, axis=0, keepdims=True), jnp.sum(upstream, axis=0, keepdims=True)


def gelu_both(u):
    bell = jnp.exp(u * u * -0.5)
    t = 1.0 / (1.0 + jnp.abs(u) * (0.3275911 * 0.7071067811865476))
    poly = 0.5 * 1.061405429 * t - 0.5 * 1.453152027
    for c in (1.421413741, -0.284496736, 0.254829592):
        poly = poly * t + 0.5 * c
    tail = poly * t * bell
    cdf = jnp.where(u >= 0, 1.0 - tail, tail)
    return u * cdf, cdf + u * bell * 0.3989422804014327


def interleave(size):
    out = lax.broadcasted_iota(jnp.int32, (size, size), 0)
    come = lax.broadcasted_iota(jnp.int32, (size, size), 1)
    quarter = size // 4
    return jnp.where((out % quarter) * 4 + out // quarter == come, 1.0, 0.0).astype(BF)


def ffn_fwd_body(at, moves, emit, words, ins, raw_in, outs, raw, own):
    a_ref, res_ref, w_ref, vec_ref = ins
    h_ref, gp_ref, v_ref, low_ref, wup_ref = outs
    tokens = a_ref.shape[0]
    order = interleave(256)
    moves.ready(w_ref)
    for g in range(FF // 256):
        block = dot(order, matrix(w_ref, g * 256, 256)).astype(BF)
        for k in range(4):
            wup_ref[k, g * 64 : (g + 1) * 64, :] = block[k * 64 : (k + 1) * 64]
    emit(wup_ref)
    moves.ready(vec_ref)
    gain, bias = vec_ref[at : at + 1, :], vec_ref[at + 1 : at + 2, :]
    for i in range(tokens // ROWS):
        rows = rows_of(i)
        moves.ready(a_ref, res_ref, tile=i)
        a = a_ref[rows, :]
        low = a.astype(BF)
        total = a + res_ref[rows, :].astype(F32)
        for k in range(4):
            lanes = slice(k * D, (k + 1) * D)
            act, slope = gelu_both(dot(low, wup_ref[k]))
            act = act.astype(BF)
            h_ref[rows, lanes] = act
            gp_ref[rows, lanes] = slope.astype(BF)
            total = total + dot(act, matrix(w_ref, FF + k * D, D))
        v_ref[rows, :] = total
        low_ref[rows, :] = normed(total, gain, bias).astype(BF)
        emit(low_ref, v_ref, h_ref, gp_ref, tile=i)


def ffn_fwd(at, base, a, res, w, vecs):
    t = a.shape[0]
    return call(
        functools.partial(ffn_fwd_body, at),
        (),
        (a, res, part_of(w, base, 2 * FF), vecs),
        [((t, FF), BF), ((t, FF), BF), ((t, D), F32), ((t, D), BF), ((4, D, D), BF)],
        [],
        [],
        12,
        tiled=2,
    )


def ffn_bwd_body(at, before, plan, base, seal, count, moves, emit, words, ins, raw_in, outs, raw, own):
    e_ref, v_ref, gp_ref, pre_ref, down_ref, wup_ref, vec_ref, h_ref, low_ref, *others = ins
    sink_refs, (first_ref, dgb_ref, ds_ref, dp_ref) = outs[:count], outs[count:]
    du_ref, dsl_ref, dk_ref = own
    sinks = sinks_of(plan, sink_refs)
    tokens = v_ref.shape[0]
    moves.ready(down_ref, wup_ref, vec_ref)
    gain, gain_pre = vec_ref[at : at + 1, :], vec_ref[before : before + 1, :]

    sums = (jnp.zeros((1, D), F32),) * 4
    for i in range(tokens // ROWS):
        rows = rows_of(i)
        moves.ready(e_ref, v_ref, gp_ref, pre_ref, tile=i)
        grad, dg, db = norm_back(v_ref[rows, :], gain, e_ref[rows, :].astype(F32))
        ds_ref[rows, :] = grad
        gl = grad.astype(BF)
        dsl_ref[rows, :] = gl
        for k in range(4):
            lanes = slice(k * D, (k + 1) * D)
            du = (dot(gl, matrix(down_ref, k * D, D), NT) * gp_ref[rows, lanes].astype(F32)).astype(BF)
            du_ref[rows, lanes] = du
            grad = grad + dot(du, wup_ref[k], NT)
        grad, dg_pre, db_pre = norm_back(pre_ref[rows, :], gain_pre, grad)
        dp_ref[rows, :] = grad
        emit(dp_ref, ds_ref, tile=i)
        sums = tuple(c + d for c, d in zip(sums, (dg_pre, db_pre, dg, db)))

    vectors = jnp.concatenate([*sums, jnp.zeros((12, D), F32)], axis=0)
    dgb_ref[...] = vectors
    if others:
        moves.ready(*others)
        vectors = jnp.concatenate([vectors[:4], others[0][:12, :]], axis=0)
    if seal is not None:
        put_all(sinks, seal, vectors.astype(BF))
    emit(dgb_ref)
    moves.ready(h_ref, low_ref)
    for k in range(8):
        piece = dot(h_ref[:, k * 256 : (k + 1) * 256], dsl_ref[...], TN).astype(BF)
        put_all(sinks, base + FF + k * 256, piece)
    for k in range(4):
        for half in range(2):
            lanes = slice(half * 256, (half + 1) * 256)
            dk_ref[k, lanes, :] = dot(low_ref[:, lanes], du_ref[:, k * D : (k + 1) * D], TN).astype(BF)
    order = interleave(256)
    for g in range(FF // 256):
        block = jnp.concatenate([dk_ref[k, g * 64 : (g + 1) * 64, :] for k in range(4)], axis=0)
        piece = dot(order, block, TN).astype(BF)
        put_all(sinks, base + g * 256, piece)
        if g == 0:
            first_ref[...] = piece[:16]
    emit(first_ref, *sink_refs)


def ffn_bwd(at, before, plan, base, e, v, h, gp, low, pre, wup, w, vecs, *others, seal=None):
    t = v.shape[0]
    shapes = sink_shapes(plan)
    outs = call(
        functools.partial(ffn_bwd_body, at, before, plan, base, seal, len(shapes)),
        (),
        (e, v, gp, pre, part_of(w, base + FF, FF), wup, vecs, h, low, *others),
        [*shapes, ((16, D), BF), ((16, D), F32), ((t, D), F32), ((t, D), F32)],
        [],
        [pltpu.VMEM((t, FF), BF), pltpu.VMEM((t, D), BF), pltpu.VMEM((4, D, D), BF)],
        13,
        tiled=4,
    )
    return outs[: len(shapes)], *outs[len(shapes) :]


def attn_fwd_body(kind, at, moves, emit, words, ins, raw_in, outs, raw, own):
    lq_ref, lk_ref = words
    xq_ref, xk_ref, w_ref, vec_ref = ins if kind == "cross" else (ins[0], *ins)
    q_ref, k_ref, v_ref, o_ref, pre_ref, out_ref, low_ref, lse_ref = outs
    (segk_ref,) = own
    tokens = q_ref.shape[0]
    blocks, width = tokens // TILE, WIDTH[kind]
    ends_q, ends_k = ends_of(lq_ref), ends_of(lk_ref)
    segk_ref[...] = seg_iota(ends_k, (8, tokens), 1)
    low = half_lanes(TILE)
    moves.ready(w_ref)
    for i in range(tokens // ROWS):
        rows = rows_of(i)
        moves.ready(xq_ref, xk_ref, tile=i)
        xq, xk = xq_ref[rows, :].astype(BF), xk_ref[rows, :].astype(BF)
        q_ref[rows, :] = dot(xq, matrix(w_ref, 0, D)).astype(BF)
        k_ref[rows, :] = dot(xk, matrix(w_ref, D, D)).astype(BF)
        v_ref[rows, :] = dot(xk, matrix(w_ref, 2 * D, D)).astype(BF)
    emit(q_ref, k_ref, v_ref)

    def one(tile, start, width, with_logs):
        rows = row_tile(tile, TILE)
        seg_q = seg_iota(ends_q, (TILE, TILE), 0, tile * TILE)
        biases = []
        for b in range(width // TILE):
            ok = seg_q == segk_ref[0:1, pl.ds(aligned(start + b * TILE), TILE)]
            if kind == "causal":
                gap = lax.broadcasted_iota(jnp.int32, (TILE, TILE), 0) - lax.broadcasted_iota(jnp.int32, (TILE, TILE), 1)
                ok = ok & (gap >= start + b * TILE - tile * TILE)
            biases.append(jnp.where(ok, 0.0, LOWEST))
        bias_q = jnp.concatenate(biases, axis=1)
        bias_q = jnp.concatenate([bias_q, bias_q], axis=0)
        outs = []
        lane = lax.broadcasted_iota(jnp.int32, (TILE, TILE), 1)
        logs = jnp.zeros((TILE, TILE), F32)
        for p in range(D // TILE):
            lanes = slice(p * TILE, (p + 1) * TILE)
            q2 = two_heads(q_ref[rows, lanes].astype(F32) * 0.125, low).astype(BF)
            s = dot(q2, k_ref[pl.ds(start, width), lanes], NT) + bias_q
            top = jnp.max(s, axis=1, keepdims=True)
            e = jnp.exp(s - top).astype(BF)
            vx = jnp.concatenate([v_ref[pl.ds(start, width), lanes], jnp.ones((width, TILE), BF)], axis=1)
            o2 = dot(e, vx)
            if with_logs:
                log = top + jnp.log(o2[:, TILE:])
                logs = jnp.where(lane == 2 * p, log[:TILE], jnp.where(lane == 2 * p + 1, log[TILE:], logs))
            o2 = o2[:, :TILE] / o2[:, TILE:]
            outs.append(jnp.where(low, o2[:TILE], o2[TILE:]))
        if with_logs:
            lse_ref[:, rows] = logs.T[:8, :]
        return jnp.concatenate(outs, axis=1)

    def step(tile, _):
        rows = row_tile(tile, TILE)
        start = window_start(kind, tile, blocks, ends_q, ends_k, width)
        o_ref[rows, :] = one(tile, start, width, True).astype(BF)
        tail = (blocks - 3) * TILE
        if kind == "cross":
            more = ends_q[-1] < (tile + 1) * TILE
        elif kind == "full":
            more = (tile == blocks - 3) & (ends_q[-1] < tail + TILE)
        else:
            more = (tile == blocks - 1) & (ends_q[-1] < tail + TILE)

        @pl.when(more)
        def _():
            o = one(tile, tail, 3 * TILE, False)
            if kind == "cross":
                mean = jnp.sum(v_ref[...].astype(F32), axis=0, keepdims=True) * (1.0 / tokens)
                o = jnp.where(ends_k[-1] >= tokens, jnp.broadcast_to(mean, o.shape), o)
            pad = lax.broadcasted_iota(jnp.int32, (TILE, D), 0) + tile * TILE >= ends_q[-1]
            o_ref[rows, :] = jnp.where(pad, o, o_ref[rows, :].astype(F32)).astype(BF)

        return 0

    lax.fori_loop(0, blocks, step, 0)
    emit(o_ref, lse_ref)
    moves.ready(vec_ref)
    gain, bias = vec_ref[at : at + 1, :], vec_ref[at + 1 : at + 2, :]

    for i in range(tokens // ROWS):
        rows = rows_of(i)
        total = xq_ref[rows, :].astype(F32) + dot(o_ref[rows, :], matrix(w_ref, 3 * D, D))
        pre_ref[rows, :] = total
        out = normed(total, gain, bias)
        out_ref[rows, :] = out
        low_ref[rows, :] = out.astype(BF)
        emit(out_ref, low_ref, pre_ref, tile=i)


def attn_fwd(kind, at, base, lq, lk, xq, xk, w, vecs):
    t = xq.shape[0]
    low, full = ((t, D), BF), ((t, D), F32)
    return call(
        functools.partial(attn_fwd_body, kind, at),
        (lq, lk),
        ((xq, xk) if kind == "cross" else (xq,)) + (part_of(w, base, 4 * D), vecs),
        [low, low, low, low, full, full, low, ((8, t), F32)],
        [],
        [pltpu.VMEM((8, t), jnp.int32)],
        12,
        tiled=2 if kind == "cross" else 1,
    )


def attn_bwd_body(kind, before, plan, base, seal, count, moves, emit, words, ins, raw_in, outs, raw, own):
    cross = kind == "cross"
    lq_ref, lk_ref = words
    if cross:
        ds_ref, o_ref, w_ref, lse_ref, q_ref, k_ref, v_ref, vec_ref, more_ref, xq_ref, xk_ref, dgb_in_ref, next_ref = ins
        sink_refs, (first_ref, dgb_ref, dx_ref, dxk_ref) = outs[:count], outs[count:]
    else:
        ds_ref, o_ref, w_ref, lse_ref, q_ref, k_ref, v_ref, vec_ref, more_ref, xq_ref, dgb_in_ref, next_ref = ins
        xk_ref, dxk_ref = xq_ref, None
        sink_refs, (first_ref, dx_ref) = outs[:count], outs[count:]
    segq_ref, segk_ref, inner_ref, dk_acc, dv_acc, dsl_ref, g_ref, dq_ref, dk_ref, dv_ref = own
    sinks = sinks_of(plan, sink_refs)
    for source, target in zip(raw_in, sink_refs):
        pairs = source.shape[0]
        moves.fetch(source, target.at[pl.ds(target.shape[0] - pairs, pairs)])
    tokens = q_ref.shape[0]
    blocks, width = tokens // TILE, WIDTH[kind]
    ends_q, ends_k = ends_of(lq_ref), ends_of(lk_ref)
    segq_ref[...] = seg_iota(ends_q, (8, tokens), 1)
    segk_ref[...] = seg_iota(ends_k, (tokens, TILE), 0)
    dk_acc[...] = jnp.zeros_like(dk_acc)
    dv_acc[...] = jnp.zeros_like(dv_acc)
    low = half_lanes(TILE)
    moves.ready(w_ref)
    heads = lax.broadcasted_iota(jnp.int32, (16, D), 1) // (D // 8) == lax.broadcasted_iota(jnp.int32, (16, D), 0)
    heads = jnp.where(heads, 1.0, 0.0).astype(BF)
    for i in range(tokens // ROWS):
        rows = rows_of(i)
        moves.ready(ds_ref, o_ref, tile=i)
        gl = ds_ref[rows, :].astype(BF)
        dsl_ref[rows, :] = gl
        g = dot(gl, matrix(w_ref, 3 * D, D), NT).astype(BF)
        g_ref[rows, :] = g
        both = g.astype(F32) * o_ref[rows, :].astype(F32)
        coarse = both.astype(BF)
        fine = (both - coarse.astype(F32)).astype(BF)
        inner_ref[:, rows] = dot(heads, coarse, NT) + dot(heads, fine, NT)
    moves.ready(q_ref, k_ref, v_ref, lse_ref)

    def step(tile, _):
        rows = row_tile(tile, TILE)
        start = window_start(kind, tile, blocks, ends_q, ends_k, width)
        win = pl.ds(start, width)
        ok = segk_ref[win, :] == segq_ref[0:1, rows]
        if kind == "causal":
            gap = lax.broadcasted_iota(jnp.int32, (width, TILE), 1) - lax.broadcasted_iota(jnp.int32, (width, TILE), 0)
            ok = ok & (gap >= start - tile * TILE)
        mask = jnp.where(ok, 0.0, LOWEST)
        mask = jnp.concatenate([mask, mask], axis=1)
        qs, gs = q_ref[rows, :], g_ref[rows, :]
        ks, vs = k_ref[win, :], v_ref[win, :]
        lses, inners = lse_ref[:, rows], inner_ref[:, rows]
        dks, dvs, dqs = [], [], []
        for p in range(D // TILE):
            lanes = slice(p * TILE, (p + 1) * TILE)
            q2 = two_heads(qs[:, lanes].astype(F32) * 0.125, low).astype(BF)
            g2 = two_heads(gs[:, lanes].astype(F32), low).astype(BF)
            lse = jnp.concatenate([lses[2 * p : 2 * p + 1], lses[2 * p + 1 : 2 * p + 2]], axis=1)
            inner = jnp.concatenate([inners[2 * p : 2 * p + 1], inners[2 * p + 1 : 2 * p + 2]], axis=1)
            prob = jnp.exp(dot(ks[:, lanes], q2, NT) + mask - lse)
            ds = (prob * (dot(vs[:, lanes], g2, NT) - inner)).astype(BF)
            dks.append(dot(ds, q2))
            dvs.append(dot(prob.astype(BF), g2))
            dq = dot(ds, ks[:, lanes], TN)
            dqs.append(jnp.where(low, dq[:TILE], dq[TILE:]) * 0.125)
        dk_acc[win, :] += jnp.concatenate(dks, axis=1)
        dv_acc[win, :] += jnp.concatenate(dvs, axis=1)
        dq_ref[rows, :] = jnp.concatenate(dqs, axis=1).astype(BF)
        return 0

    lax.fori_loop(0, blocks, step, 0)
    moves.ready(vec_ref, more_ref)

    sums = (jnp.zeros((1, D), F32),) * 2
    for i in range(tokens // ROWS):
        rows = rows_of(i)
        dk, dv = dk_acc[rows, :].astype(BF), dv_acc[rows, :].astype(BF)
        dk_ref[rows, :], dv_ref[rows, :] = dk, dv
        from_q = ds_ref[rows, :] + dot(dq_ref[rows, :], matrix(w_ref, 0, D), NT)
        from_k = dot(dk, matrix(w_ref, D, D), NT) + dot(dv, matrix(w_ref, 2 * D, D), NT)
        if not cross:
            dx_ref[rows, :] = more_ref[rows, :] + from_q + from_k
            emit(dx_ref, tile=i)
            continue
        dxk_ref[rows, :] = from_k
        grad, dg, db = norm_back(more_ref[rows, :], vec_ref[before : before + 1, :], from_q)
        dx_ref[rows, :] = grad
        emit(dx_ref, dxk_ref, tile=i)
        sums = sums[0] + dg, sums[1] + db
    moves.ready(dgb_in_ref)
    if cross:
        dgb_ref[...] = jnp.concatenate([*sums, dgb_in_ref[:14, :]], axis=0)
        emit(dgb_ref)
    moves.ready_all()
    for m, (left_ref, right_ref) in enumerate(((xq_ref, dq_ref), (xk_ref, dk_ref), (xk_ref, dv_ref), (o_ref, dsl_ref))):
        for half in range(2):
            piece = dot(left_ref[:, half * 256 : (half + 1) * 256], right_ref[...], TN).astype(BF)
            put_all(sinks, base + m * D + half * 256, piece)
            if m == half == 0:
                first_ref[...] = piece[:16]
    if plan[0] == "owned" and (base + 4 * D) % plan[1] == 0:
        sinks[0].store((base + 4 * D) // plan[1] - 1, plan[1], next_ref[...])
    emit(first_ref, *sink_refs)


def attn_bwd(kind, before, plan, base, lq, lk, ds, q, k, v, o, lse, xq, xk, w, vecs, more, dgb, following, taken=()):
    t = xq.shape[0]
    low, full = ((t, D), BF), ((t, D), F32)
    vm = pltpu.VMEM
    shapes = sink_shapes(plan)
    scratch = [vm((8, t), jnp.int32), vm((t, TILE), jnp.int32), vm((16, t), F32), vm(*full), vm(*full)] + [vm(*low)] * 5
    outs = call(
        functools.partial(attn_bwd_body, kind, before, plan, base, None, len(shapes)),
        (lq, lk),
        (ds, o, part_of(w, base, 4 * D), lse, q, k, v, vecs, more)
        + ((xq, xk) if kind == "cross" else (xq,))
        + (dgb, following),
        [*shapes, ((16, D), BF)] + ([((16, D), F32), full, full] if kind == "cross" else [full]),
        [],
        scratch,
        26,
        raw_ins=taken,
        tiled=2,
    )
    return outs[: len(shapes)], *outs[len(shapes) :]


SIDES = {"z": 4, "y": 2, "x": 2, "core": 2}
STRIDE = {"z": 8, "y": 4, "x": 2, "core": 1}


def place_of(name):
    return lax.axis_index("fsdp") // STRIDE[name] % SIDES[name]


def shifted(block, name, step, n=32):
    side, stride = SIDES[name], STRIDE[name]
    pairs = []
    for device in range(n):
        at = device // stride % side
        pairs.append((device, device + ((at + step) % side - at) * stride))
    return lax.ppermute(block, "fsdp", pairs)


def widen(pieces, name):
    if len(pieces) > 1 and name != "core":
        pieces = [(jnp.concatenate([p for p, _ in pieces]), sum((l for _, l in pieces), []))]
    spot = list(SIDES).index(name)
    more = []
    for held, labels in pieces:
        for step in range(1, SIDES[name]):
            moved = [tuple(v + step * (i == spot) for i, v in enumerate(label)) for label in labels]
            more.append((shifted(held, name, step), moved))
    return pieces + more


def after(pieces, *others):
    held = lax.optimization_barrier((*(p for p, _ in pieces), *others))
    return [(p, l) for p, (_, l) in zip(held, pieces)]


def at_home(own):
    return [(own[None], [(0, 0, 0, 0)])]


def assemble_body(spans, labels, rows, vectors, keep, *refs):
    *pieces, rows_ref, vecs_ref, land, tails, tails32, row_sem, tail_sem, out_sem, vec_sem = refs
    n = land.shape[0]
    me = lax.axis_index("fsdp")
    z, y, x, core = me // 8, me // 4 % 2, me // 2 % 2, me % 2
    for piece, (first, last), names in zip(pieces, spans, labels):
        for at, (dz, dy, dx, dc) in enumerate(names):
            owner = (((z + 4 - dz) % 4 * 2 + (y + dy) % 2) * 2 + (x + dx) % 2) * 2 + (core + dc) % 2
            whole = min(last, rows) - first
            if whole > 0:
                pltpu.make_async_copy(
                    piece.at[at, pl.ds(0, whole)], land.at[owner, pl.ds(first, whole)], row_sem
                ).start()
            if last > rows:
                pltpu.make_async_copy(
                    piece.at[at, pl.ds(whole, last - rows)], tails.at[owner], tail_sem
                ).start()
    pltpu.make_async_copy(land, land, row_sem).wait()
    pltpu.make_async_copy(tails, tails, tail_sem).wait()
    spill = lax.broadcasted_iota(jnp.int32, (16, D), 0) < vectors
    for owner in range(1, n):
        tail = jnp.where(spill, tails[owner - 1].astype(F32), 0.0)
        land[owner, 0:16] = (land[owner, 0:16].astype(F32) + tail).astype(BF)
    tails32[...] = tails[n - 1].astype(F32)
    target = rows_ref.at[:, pl.ds(0, rows)] if keep else rows_ref
    out = pltpu.make_async_copy(land, target, out_sem)
    vec = pltpu.make_async_copy(tails32, vecs_ref, vec_sem)
    out.start()
    vec.start()
    out.wait()
    vec.wait()


def assemble(parts, n, rows, vectors, keep):
    pieces, spans, labels = [], [], []
    for first, last, held in parts:
        for piece, names in held:
            pieces.append(piece)
            spans.append((first, last))
            labels.append(names)
    anywhere = pl.BlockSpec(memory_space=pl.ANY)
    return pl.pallas_call(
        functools.partial(assemble_body, spans, labels, rows, vectors, keep),
        out_shape=(jax.ShapeDtypeStruct((n, rows + 16 * keep, D), BF), jax.ShapeDtypeStruct((16, D), F32)),
        in_specs=[anywhere] * len(pieces),
        out_specs=(anywhere, anywhere),
        scratch_shapes=[
            pltpu.VMEM((n, rows, D), BF), pltpu.VMEM((n, 16, D), BF), pltpu.VMEM((16, D), F32)
        ] + [pltpu.SemaphoreType.DMA] * 4,
        cost_estimate=pl.CostEstimate(flops=int(8e10), bytes_accessed=2**20, transcendentals=0),
        compiler_params=pltpu.CompilerParams(vmem_limit_bytes=56 * 2**20),
    )(*pieces)


def geometry(local, n, vectors):
    rows = (local * n // D - vectors) // n
    return rows, rows + 16


def own_rows(flat, vectors, n):
    local = flat.shape[0]
    rows, block = geometry(local, n, vectors)
    extra = vectors * D // n
    room = jnp.pad(flat, (vectors * D, block * D - local))
    return lax.dynamic_slice(room, (vectors * D - extra * lax.axis_index("fsdp"),), (block * D,)).reshape(block, D)


def gather_whole(own, vectors, n):
    block = own.shape[0]
    rows = block - 16
    full = lax.all_gather(own, "fsdp", axis=0, tiled=True).reshape(n, block, D)
    spill = jnp.arange(16)[:, None] < vectors
    tails = jnp.where(spill, full[:-1, rows:], 0)
    return full.at[1:, :16].add(tails), full[-1, rows:].astype(F32)


def gather_plain(own, vectors, n):
    full, vecs = gather_whole(own, vectors, n)
    return full[:, : own.shape[0] - 16].reshape(-1, D), vecs


def pick(array, at, axis):
    return lax.dynamic_index_in_dim(array, at, axis, keepdims=False)


def total_of(terms):
    return sum(t.astype(F32) for t in terms)


def hold(value, *others):
    return lax.optimization_barrier((value, *others))[0]


def begin_plane(kept, sent):
    return [a.reshape(-1, 2, 2, *a.shape[1:]) for a in (kept, shifted(sent, "core", 1))]


def halve(terms, name, axis, aways=None):
    at = place_of(name)
    away = total_of([pick(t, 1 - at, axis) for t in terms]).astype(BF)
    if aways is not None:
        aways.append(away)
    return [pick(t, at, axis) for t in terms] + [shifted(away, name, 1)]


def first_ways(terms, aways=None):
    half = terms[0].shape[-2] // 32 * 16
    return (
        halve([t[..., :half, :] for t in terms], "x", 2, aways),
        halve([t[..., half:, :] for t in terms], "y", 1, aways),
    )


def second_ways(ways):
    one, two = halve(ways[0], "y", 1), halve(ways[1], "x", 1)
    return [jnp.concatenate([a, b], axis=1) for a, b in zip(one, two)]


def send_line(planes, base):
    count = planes[0].shape[0]
    z = place_of("z")
    sums = total_of(planes).astype(BF)
    pieces = []
    for step in (1, 2, 3):
        pairs = []
        for device in range(32):
            goal = (device // 8 + step) % 4
            if base <= goal < base + count:
                pairs.append((device, goal * 8 + device % 8))
        away = pick(sums, jnp.clip((z + step) % 4 - base, 0, count - 1), 0)
        pieces.append(lax.ppermute(away, "fsdp", pairs))
    return pieces


def end_line(planes, pieces, base):
    at = jnp.clip(place_of("z") - base, 0, planes[0].shape[0] - 1)
    return total_of([pick(t, at, 0) for t in planes] + pieces)


def own_part(own, vectors, local, n):
    return lax.dynamic_slice(own.reshape(-1), (vectors * D // n * lax.axis_index("fsdp"),), (local,))


def scatter_plain(matrices, vectors_sum, n):
    rows = matrices.shape[0] // n
    blocks = matrices.reshape(n, rows, D)
    tails = jnp.concatenate([blocks[1:, :16], vectors_sum[None].astype(BF)], axis=0)
    terms = jnp.concatenate([blocks, tails], axis=1).reshape(-1, D)
    return lax.psum_scatter(terms, "fsdp", scatter_dimension=0, tiled=True).astype(F32)


def on_device(src, tgt, ls, lt, enc_weights, dec_weights, cotangent, n):
    split = n == 32
    e_own, d_own = own_rows(enc_weights, 4, n), own_rows(dec_weights, 6, n)
    if split:
        b, c = at_home(e_own[:64]), at_home(e_own[64:])
        c, b = widen(c, "z"), widen(b, "y")
        b = widen(b, "z")
        w = after(at_home(d_own), *(p for p, _ in b))
        one, two = [(p[:, :64], l) for p, l in c], [(p[:, 64:], l) for p, l in c]
        one, two, w = widen(one, "x"), widen(two, "y"), widen(w, "z")
        b, one, two = widen(b, "x"), widen(one, "y"), widen(two, "x")
        b = after(b, *(p for p, _ in w))
        ready = [(0, 64, widen(b, "core")), (64, 128, widen(one, "core")), (128, 208, widen(two, "core"))]
        e_all, ev = assemble(ready, n, 192, 4, 0)
        e_all = e_all.reshape(-1, D)
        low, high = [(p[:, :144], l) for p, l in w], [(p[:, 144:], l) for p, l in w]
        low, high = widen(low, "x"), widen(high, "y")
        low, high = after(low, ev), after(high, ev)
        low, high = widen(low, "y"), widen(high, "x")
    else:
        e_all, ev = gather_plain(e_own, 4, n)
        d_all, dv = gather_plain(d_own, 6, n)
    q1, k1, v1, o1, pre1, ax, axl, lse1 = attn_fwd("full", 0, 0, ls, ls, src, src, e_all, ev)
    if split:
        low, high = after(low, axl), after(high, axl)
        low, high = widen(low, "core"), widen(high, "core")
        ax = hold(ax, *(p for p, _ in low[:2]), *(p for p, _ in high[:2]))
    hx, gpx, sum2, enc, wup_e = ffn_fwd(2, FF, ax, src, e_all, ev)
    if split:
        low, high = after(low, enc), after(high, enc)
        d_all, dv = assemble([(0, 144, low), (144, 272, high)], n, 256, 6, 1)
    q3, k3, v3, o3, pre3, h1, h1l, lse3 = attn_fwd("causal", 0, 0, lt, lt, tgt, tgt, d_all, dv)
    q4, k4, v4, o4, pre4, h2, h2l, lse4 = attn_fwd("cross", 2, FF, lt, ls, h1, enc, d_all, dv)
    hy, gpy, sum5, final, wup_d = ffn_fwd(4, 2 * FF, h2, tgt, d_all, dv)
    if split:
        d_plan = [("owned", 256, ((16, 16),)), ("owned", 256, ((8, 8),)), ("owned", 256, ((0, 8),))]
        e_plan = [("owned", 192, ((16, 16), (10, 6))), ("owned", 192, ((0, 16),))]
    else:
        d_plan = [("plain", 2 * FF, 2 * FF), ("plain", FF, FF), ("plain", 0, FF)]
        e_plan = [("plain", FF, 2 * FF), ("plain", 0, FF)]
    g3, first3, dgb, ds5, ds4 = ffn_bwd(4, 2, d_plan[0], 2 * FF, cotangent, sum5, hy, gpy, h2l, pre4, wup_d, d_all, dv)
    if split:
        p23 = begin_plane(*g3)
        p23 = halve(p23, "x", 2)
        ds4 = hold(ds4, *p23[:-1])
    g2, first2, dgb, ds3, denc = attn_bwd(
        "cross", 0, d_plan[1], FF, lt, ls, ds4, q4, k4, v4, o4, lse4, h1l, enc, d_all, dv, pre3, dgb, first3
    )
    if split:
        p23[-1], ds3, *g2 = lax.optimization_barrier((p23[-1], ds3, *g2))
        p1 = begin_plane(*g2)
        p23, p1 = halve(p23, "y", 1), halve(p1, "y", 1)
        ds3 = hold(ds3, *p23[:-1], *p1[:-1])
    g1, _, tgt_grad = attn_bwd(
        "causal", 0, d_plan[2], 0, lt, lt, ds3, q3, k3, v3, o3, lse3, tgt, tgt, d_all, dv, ds5, dgb, first2
    )
    if split:
        p23[-1], p1[-1], denc, *g1 = lax.optimization_barrier((p23[-1], p1[-1], denc, *g1, tgt_grad))[:5]
        p0 = begin_plane(*g1)
        p1, p0 = halve(p1, "x", 1), halve(p0, "x", 2)
        denc = hold(denc, *p1[:-1], *p0[:-1])
    seal = 3 * FF if split else None
    f, first, egb, ds2, ds1 = ffn_bwd(2, 0, e_plan[0], FF, denc, sum2, hx, gpx, axl, pre1, wup_e, e_all, ev, dgb, seal=seal)
    if split:
        p1[-1], p0[-1], ds1, *f = lax.optimization_barrier((p1[-1], p0[-1], ds1, *f))
        e23 = begin_plane(*f[:2])
        p0, e23 = halve(p0, "y", 1), first_ways(e23)
        ds1 = hold(ds1, *p0[:-1])
    a, _, src_grad = attn_bwd(
        "full", 0, e_plan[1], 0, ls, ls, ds1, q1, k1, v1, o1, lse1, src, src, e_all, ev, ds2, egb, first, f[2:]
    )
    if split:
        aways = []
        e01 = first_ways(begin_plane(*a), aways)
        p0[-1], e23[0][-1], e23[1][-1] = lax.optimization_barrier((p0[-1], e23[0][-1], e23[1][-1], *aways))[:3]
        d_planes = [jnp.concatenate(t) for t in zip(p0, p1, p23)]
        dz = send_line(d_planes, 0)
        e_planes = [jnp.concatenate(t) for t in zip(second_ways(e01), second_ways(e23))]
        ez = send_line(e_planes, 0)
        d_sum = end_line(d_planes, dz, 0)
        e_sum = end_line(e_planes, ez, 0)
        tail = jnp.where(lax.axis_index("fsdp") == n - 1, jnp.roll(e_sum[-16:], -4, axis=0), d_sum[-16:])
        d_sum = jnp.concatenate([d_sum[:-16], tail])
    else:
        vecs = lax.psum(jnp.concatenate([egb, dgb]), "fsdp")
        d_sum = scatter_plain(jnp.concatenate([g1[0], g2[0], g3[0]]), vecs[16:], n)
        e_sum = scatter_plain(jnp.concatenate([a[0], f[0]]), vecs[:16], n)
    enc_grad = own_part(e_sum, 4, enc_weights.shape[0], n)
    dec_grad = own_part(d_sum, 6, dec_weights.shape[0], n)
    return final, src_grad, tgt_grad, enc_grad, dec_grad


def solution(mesh):
    n = mesh.shape["fsdp"]
    return jax.shard_map(
        functools.partial(on_device, n=n),
        mesh=mesh,
        in_specs=(P("fsdp", None),) * 4 + (P("fsdp"),) * 2 + (P("fsdp", None),),
        out_specs=(P("fsdp", None),) * 3 + (P("fsdp"),) * 2,
        check_vma=False,
    )
```

```python
import functools
import math

import jax
import jax.numpy as jnp
from jax import lax
from jax.experimental import pallas as pl
from jax.experimental.pallas import tpu as pltpu
from jax.sharding import PartitionSpec as P

D=512; TILE=128; SENTS=16; LOWEST=-1e30
NT=(((1,),(1,)),((),())); TN=(((0,),(0,)),((),()))
BF=jnp.bfloat16; F32=jnp.float32

def aligned(at):
    return at if isinstance(at,int) else pl.multiple_of(at,TILE)

def ends_of(ref):
    ends=[]; total=ref[0,0]
    ends.append(total)
    for j in range(1,SENTS):
        total=total+ref[0,j]; ends.append(total)
    return ends

def seg_iota(ends, shape, dim, base=0):
    place=lax.broadcasted_iota(jnp.int32, shape, dim)+base
    seg=jnp.zeros(shape,jnp.int32)
    for e in ends: seg=seg+(place>=e).astype(jnp.int32)
    return seg

def start_of(pos, ends_q, ends_k):
    at=jnp.int32(0)
    for eq,ek in zip(ends_q,ends_k): at=jnp.where(pos>=eq, ek, at)
    return at

def half_lanes(rows):
    return lax.broadcasted_iota(jnp.int32,(rows,TILE),1)<TILE//2

def two_heads(block, low):
    zero=jnp.zeros_like(block)
    return jnp.concatenate([jnp.where(low,block,zero),jnp.where(low,zero,block)],axis=0)

def window_start(kind, tile, blocks, ends_q, ends_k, width):
    if kind=="cross":
        first=start_of(tile*TILE, ends_q, ends_k)//TILE
    else:
        first=tile-1
    return pl.multiple_of(jnp.clip(first,0,blocks-width//TILE)*TILE,TILE)

WIDTH={"full":384,"causal":256,"cross":512}

VM=pl.BlockSpec(memory_space=pltpu.VMEM); SM=pl.BlockSpec(memory_space=pltpu.SMEM)
FF = 2048
EPSILON = 1e-05

def dot(a, b, dims=(((1,), (0,)), ((), ()))):
    return lax.dot_general(a, b, dims, preferred_element_type=F32)


def row_tile(i, size):
    return pl.ds(pl.multiple_of(i * size, size), size)


class Moves:
    def __init__(self, sems):
        self.sems, self.used, self.coming, self.going = sems, 0, [], []

    def copy(self, source, target):
        made = pltpu.make_async_copy(source, target, self.sems.at[self.used])
        self.used += 1
        made.start()
        return made

    def fetch(self, source, target, tile=None):
        self.coming.append((target, tile, self.copy(source, target if tile is None else target.at[rows_of(tile)])))

    def ready(self, *refs, tile=None):
        left = []
        for entry in self.coming:
            if any(entry[0] is ref for ref in refs) and (tile is None or entry[1] in (None, tile)):
                entry[2].wait()
            else:
                left.append(entry)
        self.coming = left

    def ready_all(self):
        for entry in self.coming:
            entry[2].wait()
        self.coming = []

    def send(self, source, target):
        self.going.append(self.copy(source, target))

    def finish(self):
        self.ready_all()
        for made in self.going:
            made.wait()


ROWS = 512


def rows_of(tile):
    return slice(tile * ROWS, (tile + 1) * ROWS)


def call(body, scalars, ins, outs, raw_outs, scratch, micros, raw_ins=(), alias=False, tiled=0):
    ins = [a if isinstance(a, tuple) else (a, 0, a.shape[0]) for a in ins]
    tall = [(count, *a.shape[1:]) for a, _, count in ins]
    tiles = tall[0][0] // ROWS if tiled else 1

    def kernel(*refs):
        refs = list(refs)

        def cut(count):
            taken = refs[:count]
            del refs[:count]
            return taken

        words, sources, raw_in, targets, raw = (
            cut(len(scalars)), cut(len(ins)), cut(len(raw_ins)), cut(len(outs)), cut(len(raw_outs))
        )
        in_refs, out_refs, own = cut(len(ins)), cut(len(outs)), cut(len(scratch))
        moves = Moves(refs[0])
        pairs = list(zip(sources, in_refs, ins))
        for tile in range(tiles):
            for source, target, _ in pairs[:tiled]:
                moves.fetch(source.at[rows_of(tile)], target, tile)
            if tile == 0:
                for source, target, (_, first, count) in pairs[tiled:]:
                    moves.fetch(source.at[pl.ds(first, count)], target)
        place = {id(ref): target for ref, target in zip(out_refs, targets)}

        def emit(*done, tile=None):
            for ref in done:
                if id(ref) not in place:
                    continue
                part = (lambda r: r) if tile is None else (lambda r: r.at[rows_of(tile)])
                moves.send(part(ref), part(place[id(ref)]))

        body(moves, emit, words, in_refs, raw_in, out_refs, raw, own)
        moves.finish()

    anywhere = pl.BlockSpec(memory_space=pl.ANY)
    held = [*((s, a.dtype) for s, (a, _, _) in zip(tall, ins)), *outs]
    room = sum(math.prod(s) * jnp.dtype(d).itemsize for s, d in held)
    room += sum(math.prod(s.shape) * jnp.dtype(s.dtype).itemsize for s in scratch)
    return pl.pallas_call(
        kernel,
        out_shape=tuple(jax.ShapeDtypeStruct(s, d) for s, d in (*outs, *raw_outs)),
        in_specs=[SM] * len(scalars) + [anywhere] * (len(ins) + len(raw_ins)),
        out_specs=(anywhere,) * (len(outs) + len(raw_outs)),
        scratch_shapes=[
            *(pltpu.VMEM(s, d) for s, d in held),
            *scratch,
            pltpu.SemaphoreType.DMA((len(ins) + tiled * (tiles - 1) + len(outs) * tiles + 8,)),
        ],
        input_output_aliases={len(scalars) + len(ins): len(outs)} if alias else {},
        cost_estimate=pl.CostEstimate(flops=int(micros * 1e10), bytes_accessed=2**20, transcendentals=0),
        compiler_params=pltpu.CompilerParams(vmem_limit_bytes=max(room + 8 * 2**20, 56 * 2**20)),
    )(*scalars, *(a for a, _, _ in ins), *raw_ins)


class Plain:
    def __init__(self, base, ref):
        self.base, self.ref = base, ref

    def put(self, first, value):
        if first - self.base < self.ref.shape[0]:
            self.ref[first - self.base : first - self.base + value.shape[0], :] = value


class Laid:
    def __init__(self, rows, base, ref):
        self.rows, self.base, self.ref = rows, base, ref

    def put(self, first, value):
        last = first + value.shape[0]
        for owner in range(first // self.rows, (last - 1) // self.rows + 1):
            low, high = max(first, owner * self.rows), min(last, (owner + 1) * self.rows)
            self.store(owner, low - owner * self.rows, value[low - first : high - first])
            if low == owner * self.rows:
                self.store(owner - 1, self.rows, value[low - first : low - first + 16])

    def store(self, owner, at, value):
        if 0 <= owner - self.base < self.ref.shape[0]:
            self.ref[owner - self.base, at : at + value.shape[0], :] = value


class Owned(Laid):
    def __init__(self, rows, base, kept, sent):
        self.rows, self.base, self.kept, self.sent = rows, base, kept, sent
        self.core = lax.axis_index("fsdp") % 2

    def store(self, owner, at, value):
        pair = (owner - self.base) // 2
        if not 0 <= pair < self.kept.shape[0]:
            return

        @pl.when(self.core == owner % 2)
        def _():
            self.kept[pair, at : at + value.shape[0], :] = value

        @pl.when(self.core != owner % 2)
        def _():
            self.sent[pair, at : at + value.shape[0], :] = value


def sinks_of(plan, refs):
    if plan[0] == "plain":
        return [Plain(plan[1], refs[0])]
    if plan[0] == "laid":
        return [Laid(plan[1], plan[2], refs[0])]
    return [Owned(plan[1], base, refs[2 * i], refs[2 * i + 1]) for i, (base, _) in enumerate(plan[2])]


def sink_shapes(plan):
    if plan[0] == "plain":
        return [((plan[2], D), BF)]
    if plan[0] == "laid":
        return [((plan[3], plan[1] + 16, D), BF)]
    return [((owners // 2, plan[1] + 16, D), BF) for _, owners in plan[2] for _ in range(2)]


def put_all(sinks, first, value):
    for sink in sinks:
        sink.put(first, value)


def matrix(ref, first, rows):
    if len(ref.shape) == 2:
        return ref[first : first + rows, :]
    each = ref.shape[1] - 16
    return ref[first // each : (first + rows) // each, :each, :].reshape(rows, D)


def part_of(w, first, rows):
    each = 1 if len(w.shape) == 2 else w.shape[1] - 16
    return w, first // each, rows // each


def normed(values, gain, bias):
    center = jnp.mean(values, axis=1, keepdims=True)
    shifted = values - center
    spread = jnp.mean(shifted * shifted, axis=1, keepdims=True)
    return shifted * lax.rsqrt(spread + EPSILON) * gain + bias


def norm_back(values, gain, upstream):
    center = jnp.mean(values, axis=1, keepdims=True)
    shifted = values - center
    r = lax.rsqrt(jnp.mean(shifted * shifted, axis=1, keepdims=True) + EPSILON)
    hat = shifted * r
    scaled = upstream * gain
    inner = jnp.mean(scaled * hat, axis=1, keepdims=True)
    grad = r * (scaled - jnp.mean(scaled, axis=1, keepdims=True) - hat * inner)
    return grad, jnp.sum(upstream * hat, axis=0, keepdims=True), jnp.sum(upstream, axis=0, keepdims=True)


def gelu_both(u):
    bell = jnp.exp(u * u * -0.5)
    t = 1.0 / (1.0 + jnp.abs(u) * (0.3275911 * 0.7071067811865476))
    poly = 0.5 * 1.061405429 * t - 0.5 * 1.453152027
    for c in (1.421413741, -0.284496736, 0.254829592):
        poly = poly * t + 0.5 * c
    tail = poly * t * bell
    cdf = jnp.where(u >= 0, 1.0 - tail, tail)
    return u * cdf, cdf + u * bell * 0.3989422804014327


def interleave(size):
    out = lax.broadcasted_iota(jnp.int32, (size, size), 0)
    come = lax.broadcasted_iota(jnp.int32, (size, size), 1)
    quarter = size // 4
    return jnp.where((out % quarter) * 4 + out // quarter == come, 1.0, 0.0).astype(BF)


def ffn_fwd_body(at, moves, emit, words, ins, raw_in, outs, raw, own):
    a_ref, res_ref, w_ref, vec_ref = ins
    h_ref, gp_ref, v_ref, low_ref, wup_ref = outs
    tokens = a_ref.shape[0]
    order = interleave(256)
    moves.ready(w_ref)
    for g in range(FF // 256):
        block = dot(order, matrix(w_ref, g * 256, 256)).astype(BF)
        for k in range(4):
            wup_ref[k, g * 64 : (g + 1) * 64, :] = block[k * 64 : (k + 1) * 64]
    emit(wup_ref)
    moves.ready(vec_ref)
    gain, bias = vec_ref[at : at + 1, :], vec_ref[at + 1 : at + 2, :]
    for i in range(tokens // ROWS):
        rows = rows_of(i)
        moves.ready(a_ref, res_ref, tile=i)
        a = a_ref[rows, :]
        low = a.astype(BF)
        total = a + res_ref[rows, :].astype(F32)
        for k in range(4):
            lanes = slice(k * D, (k + 1) * D)
            act, slope = gelu_both(dot(low, wup_ref[k]))
            act = act.astype(BF)
            h_ref[rows, lanes] = act
            gp_ref[rows, lanes] = slope.astype(BF)
            total = total + dot(act, matrix(w_ref, FF + k * D, D))
        v_ref[rows, :] = total
        low_ref[rows, :] = normed(total, gain, bias).astype(BF)
        emit(low_ref, v_ref, h_ref, gp_ref, tile=i)


def ffn_bwd_body(at, before, plan, base, seal, count, moves, emit, words, ins, raw_in, outs, raw, own):
    e_ref, v_ref, gp_ref, pre_ref, down_ref, wup_ref, vec_ref, h_ref, low_ref, *others = ins
    sink_refs, (first_ref, dgb_ref, ds_ref, dp_ref) = outs[:count], outs[count:]
    du_ref, dsl_ref, dk_ref = own
    sinks = sinks_of(plan, sink_refs)
    tokens = v_ref.shape[0]
    moves.ready(down_ref, wup_ref, vec_ref)
    gain, gain_pre = vec_ref[at : at + 1, :], vec_ref[before : before + 1, :]

    sums = (jnp.zeros((1, D), F32),) * 4
    for i in range(tokens // ROWS):
        rows = rows_of(i)
        moves.ready(e_ref, v_ref, gp_ref, pre_ref, tile=i)
        grad, dg, db = norm_back(v_ref[rows, :], gain, e_ref[rows, :].astype(F32))
        ds_ref[rows, :] = grad
        gl = grad.astype(BF)
        dsl_ref[rows, :] = gl
        for k in range(4):
            lanes = slice(k * D, (k + 1) * D)
            du = (dot(gl, matrix(down_ref, k * D, D), NT) * gp_ref[rows, lanes].astype(F32)).astype(BF)
            du_ref[rows, lanes] = du
            grad = grad + dot(du, wup_ref[k], NT)
        grad, dg_pre, db_pre = norm_back(pre_ref[rows, :], gain_pre, grad)
        dp_ref[rows, :] = grad
        emit(dp_ref, ds_ref, tile=i)
        sums = tuple(c + d for c, d in zip(sums, (dg_pre, db_pre, dg, db)))

    vectors = jnp.concatenate([*sums, jnp.zeros((12, D), F32)], axis=0)
    dgb_ref[...] = vectors
    if others:
        moves.ready(*others)
        vectors = jnp.concatenate([vectors[:4], others[0][:12, :]], axis=0)
    if seal is not None:
        put_all(sinks, seal, vectors.astype(BF))
    emit(dgb_ref)
    moves.ready(h_ref, low_ref)
    for k in range(8):
        piece = dot(h_ref[:, k * 256 : (k + 1) * 256], dsl_ref[...], TN).astype(BF)
        put_all(sinks, base + FF + k * 256, piece)
    for k in range(4):
        for half in range(2):
            lanes = slice(half * 256, (half + 1) * 256)
            dk_ref[k, lanes, :] = dot(low_ref[:, lanes], du_ref[:, k * D : (k + 1) * D], TN).astype(BF)
    order = interleave(256)
    for g in range(FF // 256):
        block = jnp.concatenate([dk_ref[k, g * 64 : (g + 1) * 64, :] for k in range(4)], axis=0)
        piece = dot(order, block, TN).astype(BF)
        put_all(sinks, base + g * 256, piece)
        if g == 0:
            first_ref[...] = piece[:16]
    emit(first_ref, *sink_refs)


def ffn_bwd(at, before, plan, base, e, v, h, gp, low, pre, wup, w, vecs, *others, seal=None):
    t = v.shape[0]
    shapes = sink_shapes(plan)
    outs = call(
        functools.partial(ffn_bwd_body, at, before, plan, base, seal, len(shapes)),
        (),
        (e, v, gp, pre, part_of(w, base + FF, FF), wup, vecs, h, low, *others),
        [*shapes, ((16, D), BF), ((16, D), F32), ((t, D), F32), ((t, D), F32)],
        [],
        [pltpu.VMEM((t, FF), BF), pltpu.VMEM((t, D), BF), pltpu.VMEM((4, D, D), BF)],
        13,
        tiled=4,
    )
    return outs[: len(shapes)], *outs[len(shapes) :]


def attn_fwd_body(kind, at, moves, emit, words, ins, raw_in, outs, raw, own):
    lq_ref, lk_ref = words
    xq_ref, xk_ref, w_ref, vec_ref = ins if kind == "cross" else (ins[0], *ins)
    q_ref, k_ref, v_ref, o_ref, pre_ref, out_ref, low_ref, lse_ref = outs
    (segk_ref,) = own
    tokens = q_ref.shape[0]
    blocks, width = tokens // TILE, WIDTH[kind]
    ends_q, ends_k = ends_of(lq_ref), ends_of(lk_ref)
    segk_ref[...] = seg_iota(ends_k, (8, tokens), 1)
    low = half_lanes(TILE)
    moves.ready(w_ref)
    for i in range(tokens // ROWS):
        rows = rows_of(i)
        moves.ready(xq_ref, xk_ref, tile=i)
        xq, xk = xq_ref[rows, :].astype(BF), xk_ref[rows, :].astype(BF)
        q_ref[rows, :] = dot(xq, matrix(w_ref, 0, D)).astype(BF)
        k_ref[rows, :] = dot(xk, matrix(w_ref, D, D)).astype(BF)
        v_ref[rows, :] = dot(xk, matrix(w_ref, 2 * D, D)).astype(BF)
    emit(q_ref, k_ref, v_ref)

    def one(tile, start, width, with_logs):
        rows = row_tile(tile, TILE)
        seg_q = seg_iota(ends_q, (TILE, TILE), 0, tile * TILE)
        biases = []
        for b in range(width // TILE):
            ok = seg_q == segk_ref[0:1, pl.ds(aligned(start + b * TILE), TILE)]
            if kind == "causal":
                gap = lax.broadcasted_iota(jnp.int32, (TILE, TILE), 0) - lax.broadcasted_iota(jnp.int32, (TILE, TILE), 1)
                ok = ok & (gap >= start + b * TILE - tile * TILE)
            biases.append(jnp.where(ok, 0.0, LOWEST))
        bias_q = jnp.concatenate(biases, axis=1)
        bias_q = jnp.concatenate([bias_q, bias_q], axis=0)
        outs = []
        lane = lax.broadcasted_iota(jnp.int32, (TILE, TILE), 1)
        logs = jnp.zeros((TILE, TILE), F32)
        for p in range(D // TILE):
            lanes = slice(p * TILE, (p + 1) * TILE)
            q2 = two_heads(q_ref[rows, lanes].astype(F32) * 0.125, low).astype(BF)
            s = dot(q2, k_ref[pl.ds(start, width), lanes], NT) + bias_q
            top = jnp.max(s, axis=1, keepdims=True)
            e = jnp.exp(s - top).astype(BF)
            vx = jnp.concatenate([v_ref[pl.ds(start, width), lanes], jnp.ones((width, TILE), BF)], axis=1)
            o2 = dot(e, vx)
            if with_logs:
                log = top + jnp.log(o2[:, TILE:])
                logs = jnp.where(lane == 2 * p, log[:TILE], jnp.where(lane == 2 * p + 1, log[TILE:], logs))
            o2 = o2[:, :TILE] / o2[:, TILE:]
            outs.append(jnp.where(low, o2[:TILE], o2[TILE:]))
        if with_logs:
            lse_ref[:, rows] = logs.T[:8, :]
        return jnp.concatenate(outs, axis=1)

    def step(tile, _):
        rows = row_tile(tile, TILE)
        start = window_start(kind, tile, blocks, ends_q, ends_k, width)
        o_ref[rows, :] = one(tile, start, width, True).astype(BF)
        tail = (blocks - 3) * TILE
        if kind == "cross":
            more = ends_q[-1] < (tile + 1) * TILE
        elif kind == "full":
            more = (tile == blocks - 3) & (ends_q[-1] < tail + TILE)
        else:
            more = (tile == blocks - 1) & (ends_q[-1] < tail + TILE)

        @pl.when(more)
        def _():
            o = one(tile, tail, 3 * TILE, False)
            if kind == "cross":
                mean = jnp.sum(v_ref[...].astype(F32), axis=0, keepdims=True) * (1.0 / tokens)
                o = jnp.where(ends_k[-1] >= tokens, jnp.broadcast_to(mean, o.shape), o)
            pad = lax.broadcasted_iota(jnp.int32, (TILE, D), 0) + tile * TILE >= ends_q[-1]
            o_ref[rows, :] = jnp.where(pad, o, o_ref[rows, :].astype(F32)).astype(BF)

        return 0

    lax.fori_loop(0, blocks, step, 0)
    emit(o_ref, lse_ref)
    moves.ready(vec_ref)
    gain, bias = vec_ref[at : at + 1, :], vec_ref[at + 1 : at + 2, :]

    for i in range(tokens // ROWS):
        rows = rows_of(i)
        total = xq_ref[rows, :].astype(F32) + dot(o_ref[rows, :], matrix(w_ref, 3 * D, D))
        pre_ref[rows, :] = total
        out = normed(total, gain, bias)
        out_ref[rows, :] = out
        low_ref[rows, :] = out.astype(BF)
        emit(out_ref, low_ref, pre_ref, tile=i)


def forward_body(kinds, moves, emit, words, ins, raw_in, outs, raw, own):
    *inputs, vec_ref = ins
    segk_ref, *mids = own
    at = 0
    x_ref = res_ref = inputs.pop(0)
    for i, kind in enumerate(kinds):
        lengths = (words[0], words[-1]) if kind == "cross" else (words[0], words[0])
        sources = (x_ref, inputs.pop(0)) if kind == "cross" else (x_ref,)
        low_outs = outs[7 * i : 7 * i + 7]
        attn_fwd_body(
            kind, at, moves, emit, lengths, (*sources, inputs.pop(0), vec_ref), raw_in,
            (*low_outs[:5], mids[i], *low_outs[5:]), raw, (segk_ref,)
        )
        x_ref = mids[i]
        at += 2
    ffn_fwd_body(at, moves, emit, words, (x_ref, res_ref, inputs.pop(0), vec_ref), raw_in, outs[7 * len(kinds) :], raw, ())


def forward(kinds, lengths, x, other, w, vecs):
    t = x.shape[0]
    low, full = ((t, D), BF), ((t, D), F32)
    ins = [x]
    for i, kind in enumerate(kinds):
        ins += ([other] if kind == "cross" else []) + [part_of(w, i * FF, FF)]
    return call(
        functools.partial(forward_body, kinds),
        lengths,
        (*ins, part_of(w, len(kinds) * FF, 2 * FF), vecs),
        [low, low, low, low, full, low, ((8, t), F32)] * len(kinds)
        + [((t, FF), BF), ((t, FF), BF), full, low, ((4, D, D), BF)],
        [],
        [pltpu.VMEM((8, t), jnp.int32)] + [pltpu.VMEM(*full)] * len(kinds),
        30,
    )


def attn_bwd_body(kind, before, plan, base, seal, count, moves, emit, words, ins, raw_in, outs, raw, own):
    cross = kind == "cross"
    lq_ref, lk_ref = words
    if cross:
        ds_ref, o_ref, w_ref, lse_ref, q_ref, k_ref, v_ref, vec_ref, more_ref, xq_ref, xk_ref, dgb_in_ref, next_ref = ins
        sink_refs, (first_ref, dgb_ref, dx_ref, dxk_ref) = outs[:count], outs[count:]
    else:
        ds_ref, o_ref, w_ref, lse_ref, q_ref, k_ref, v_ref, vec_ref, more_ref, xq_ref, dgb_in_ref, next_ref = ins
        xk_ref, dxk_ref = xq_ref, None
        sink_refs, (first_ref, dx_ref) = outs[:count], outs[count:]
    segq_ref, segk_ref, inner_ref, dk_acc, dv_acc, dsl_ref, g_ref, dq_ref, dk_ref, dv_ref = own
    sinks = sinks_of(plan, sink_refs)
    for source, target in zip(raw_in, sink_refs):
        pairs = source.shape[0]
        moves.fetch(source, target.at[pl.ds(target.shape[0] - pairs, pairs)])
    tokens = q_ref.shape[0]
    blocks, width = tokens // TILE, WIDTH[kind]
    ends_q, ends_k = ends_of(lq_ref), ends_of(lk_ref)
    segq_ref[...] = seg_iota(ends_q, (8, tokens), 1)
    segk_ref[...] = seg_iota(ends_k, (tokens, TILE), 0)
    dk_acc[...] = jnp.zeros_like(dk_acc)
    dv_acc[...] = jnp.zeros_like(dv_acc)
    low = half_lanes(TILE)
    moves.ready(w_ref)
    heads = lax.broadcasted_iota(jnp.int32, (16, D), 1) // (D // 8) == lax.broadcasted_iota(jnp.int32, (16, D), 0)
    heads = jnp.where(heads, 1.0, 0.0).astype(BF)
    for i in range(tokens // ROWS):
        rows = rows_of(i)
        moves.ready(ds_ref, o_ref, tile=i)
        gl = ds_ref[rows, :].astype(BF)
        dsl_ref[rows, :] = gl
        g = dot(gl, matrix(w_ref, 3 * D, D), NT).astype(BF)
        g_ref[rows, :] = g
        both = g.astype(F32) * o_ref[rows, :].astype(F32)
        coarse = both.astype(BF)
        fine = (both - coarse.astype(F32)).astype(BF)
        inner_ref[:, rows] = dot(heads, coarse, NT) + dot(heads, fine, NT)
    moves.ready(q_ref, k_ref, v_ref, lse_ref)

    def step(tile, _):
        rows = row_tile(tile, TILE)
        start = window_start(kind, tile, blocks, ends_q, ends_k, width)
        win = pl.ds(start, width)
        ok = segk_ref[win, :] == segq_ref[0:1, rows]
        if kind == "causal":
            gap = lax.broadcasted_iota(jnp.int32, (width, TILE), 1) - lax.broadcasted_iota(jnp.int32, (width, TILE), 0)
            ok = ok & (gap >= start - tile * TILE)
        mask = jnp.where(ok, 0.0, LOWEST)
        mask = jnp.concatenate([mask, mask], axis=1)
        qs, gs = q_ref[rows, :], g_ref[rows, :]
        ks, vs = k_ref[win, :], v_ref[win, :]
        lses, inners = lse_ref[:, rows], inner_ref[:, rows]
        dks, dvs, dqs = [], [], []
        for p in range(D // TILE):
            lanes = slice(p * TILE, (p + 1) * TILE)
            q2 = two_heads(qs[:, lanes].astype(F32) * 0.125, low).astype(BF)
            g2 = two_heads(gs[:, lanes].astype(F32), low).astype(BF)
            lse = jnp.concatenate([lses[2 * p : 2 * p + 1], lses[2 * p + 1 : 2 * p + 2]], axis=1)
            inner = jnp.concatenate([inners[2 * p : 2 * p + 1], inners[2 * p + 1 : 2 * p + 2]], axis=1)
            prob = jnp.exp(dot(ks[:, lanes], q2, NT) + mask - lse)
            ds = (prob * (dot(vs[:, lanes], g2, NT) - inner)).astype(BF)
            dks.append(dot(ds, q2))
            dvs.append(dot(prob.astype(BF), g2))
            dq = dot(ds, ks[:, lanes], TN)
            dqs.append(jnp.where(low, dq[:TILE], dq[TILE:]) * 0.125)
        dk_acc[win, :] += jnp.concatenate(dks, axis=1)
        dv_acc[win, :] += jnp.concatenate(dvs, axis=1)
        dq_ref[rows, :] = jnp.concatenate(dqs, axis=1).astype(BF)
        return 0

    lax.fori_loop(0, blocks, step, 0)
    moves.ready(vec_ref, more_ref)

    sums = (jnp.zeros((1, D), F32),) * 2
    for i in range(tokens // ROWS):
        rows = rows_of(i)
        dk, dv = dk_acc[rows, :].astype(BF), dv_acc[rows, :].astype(BF)
        dk_ref[rows, :], dv_ref[rows, :] = dk, dv
        from_q = ds_ref[rows, :] + dot(dq_ref[rows, :], matrix(w_ref, 0, D), NT)
        from_k = dot(dk, matrix(w_ref, D, D), NT) + dot(dv, matrix(w_ref, 2 * D, D), NT)
        if not cross:
            dx_ref[rows, :] = more_ref[rows, :] + from_q + from_k
            emit(dx_ref, tile=i)
            continue
        dxk_ref[rows, :] = from_k
        grad, dg, db = norm_back(more_ref[rows, :], vec_ref[before : before + 1, :], from_q)
        dx_ref[rows, :] = grad
        emit(dx_ref, dxk_ref, tile=i)
        sums = sums[0] + dg, sums[1] + db
    moves.ready(dgb_in_ref)
    if cross:
        dgb_ref[...] = jnp.concatenate([*sums, dgb_in_ref[:14, :]], axis=0)
        emit(dgb_ref)
    moves.ready_all()
    for m, (left_ref, right_ref) in enumerate(((xq_ref, dq_ref), (xk_ref, dk_ref), (xk_ref, dv_ref), (o_ref, dsl_ref))):
        for half in range(2):
            piece = dot(left_ref[:, half * 256 : (half + 1) * 256], right_ref[...], TN).astype(BF)
            put_all(sinks, base + m * D + half * 256, piece)
            if m == half == 0:
                first_ref[...] = piece[:16]
    if plan[0] == "owned" and (base + 4 * D) % plan[1] == 0:
        sinks[0].store((base + 4 * D) // plan[1] - 1, plan[1], next_ref[...])
    emit(first_ref, *sink_refs)


def attn_bwd(kind, before, plan, base, lq, lk, ds, q, k, v, o, lse, xq, xk, w, vecs, more, dgb, following, taken=()):
    t = xq.shape[0]
    low, full = ((t, D), BF), ((t, D), F32)
    vm = pltpu.VMEM
    shapes = sink_shapes(plan)
    scratch = [vm((8, t), jnp.int32), vm((t, TILE), jnp.int32), vm((16, t), F32), vm(*full), vm(*full)] + [vm(*low)] * 5
    outs = call(
        functools.partial(attn_bwd_body, kind, before, plan, base, None, len(shapes)),
        (lq, lk),
        (ds, o, part_of(w, base, 4 * D), lse, q, k, v, vecs, more)
        + ((xq, xk) if kind == "cross" else (xq,))
        + (dgb, following),
        [*shapes, ((16, D), BF)] + ([((16, D), F32), full, full] if kind == "cross" else [full]),
        [],
        scratch,
        26,
        raw_ins=taken,
        tiled=2,
    )
    return outs[: len(shapes)], *outs[len(shapes) :]


SIDES = {"z": 4, "y": 2, "x": 2, "core": 2}
STRIDE = {"z": 8, "y": 4, "x": 2, "core": 1}


def place_of(name):
    return lax.axis_index("fsdp") // STRIDE[name] % SIDES[name]


def shifted(block, name, step, n=32):
    side, stride = SIDES[name], STRIDE[name]
    pairs = []
    for device in range(n):
        at = device // stride % side
        pairs.append((device, device + ((at + step) % side - at) * stride))
    return lax.ppermute(block, "fsdp", pairs)


def widen(pieces, name):
    if len(pieces) > 1 and name != "core":
        pieces = [(jnp.concatenate([p for p, _ in pieces]), sum((l for _, l in pieces), []))]
    spot = list(SIDES).index(name)
    more = []
    for held, labels in pieces:
        for step in range(1, SIDES[name]):
            moved = [tuple(v + step * (i == spot) for i, v in enumerate(label)) for label in labels]
            more.append((shifted(held, name, step), moved))
    return pieces + more


def after(pieces, *others):
    held = lax.optimization_barrier((*(p for p, _ in pieces), *others))
    return [(p, l) for p, (_, l) in zip(held, pieces)]


def at_home(own):
    return [(own[None], [(0, 0, 0, 0)])]


def assemble_body(spans, labels, rows, vectors, keep, *refs):
    *pieces, rows_ref, vecs_ref, land, tails, tails32, row_sem, tail_sem, out_sem, vec_sem = refs
    n = land.shape[0]
    me = lax.axis_index("fsdp")
    z, y, x, core = me // 8, me // 4 % 2, me // 2 % 2, me % 2
    for piece, (first, last), names in zip(pieces, spans, labels):
        for at, (dz, dy, dx, dc) in enumerate(names):
            owner = (((z + 4 - dz) % 4 * 2 + (y + dy) % 2) * 2 + (x + dx) % 2) * 2 + (core + dc) % 2
            whole = min(last, rows) - first
            if whole > 0:
                pltpu.make_async_copy(
                    piece.at[at, pl.ds(0, whole)], land.at[owner, pl.ds(first, whole)], row_sem
                ).start()
            if last > rows:
                pltpu.make_async_copy(
                    piece.at[at, pl.ds(whole, last - rows)], tails.at[owner], tail_sem
                ).start()
    pltpu.make_async_copy(land, land, row_sem).wait()
    pltpu.make_async_copy(tails, tails, tail_sem).wait()
    spill = lax.broadcasted_iota(jnp.int32, (16, D), 0) < vectors
    for owner in range(1, n):
        tail = jnp.where(spill, tails[owner - 1].astype(F32), 0.0)
        land[owner, 0:16] = (land[owner, 0:16].astype(F32) + tail).astype(BF)
    tails32[...] = tails[n - 1].astype(F32)
    target = rows_ref.at[:, pl.ds(0, rows)] if keep else rows_ref
    out = pltpu.make_async_copy(land, target, out_sem)
    vec = pltpu.make_async_copy(tails32, vecs_ref, vec_sem)
    out.start()
    vec.start()
    out.wait()
    vec.wait()


def assemble(parts, n, rows, vectors, keep):
    pieces, spans, labels = [], [], []
    for first, last, held in parts:
        for piece, names in held:
            pieces.append(piece)
            spans.append((first, last))
            labels.append(names)
    anywhere = pl.BlockSpec(memory_space=pl.ANY)
    return pl.pallas_call(
        functools.partial(assemble_body, spans, labels, rows, vectors, keep),
        out_shape=(jax.ShapeDtypeStruct((n, rows + 16 * keep, D), BF), jax.ShapeDtypeStruct((16, D), F32)),
        in_specs=[anywhere] * len(pieces),
        out_specs=(anywhere, anywhere),
        scratch_shapes=[
            pltpu.VMEM((n, rows, D), BF), pltpu.VMEM((n, 16, D), BF), pltpu.VMEM((16, D), F32)
        ] + [pltpu.SemaphoreType.DMA] * 4,
        cost_estimate=pl.CostEstimate(flops=int(8e10), bytes_accessed=2**20, transcendentals=0),
        compiler_params=pltpu.CompilerParams(vmem_limit_bytes=56 * 2**20),
    )(*pieces)


def geometry(local, n, vectors):
    rows = (local * n // D - vectors) // n
    return rows, rows + 16


def own_rows(flat, vectors, n):
    local = flat.shape[0]
    rows, block = geometry(local, n, vectors)
    extra = vectors * D // n
    room = jnp.pad(flat, (vectors * D, block * D - local))
    return lax.dynamic_slice(room, (vectors * D - extra * lax.axis_index("fsdp"),), (block * D,)).reshape(block, D)


def gather_whole(own, vectors, n):
    block = own.shape[0]
    rows = block - 16
    full = lax.all_gather(own, "fsdp", axis=0, tiled=True).reshape(n, block, D)
    spill = jnp.arange(16)[:, None] < vectors
    tails = jnp.where(spill, full[:-1, rows:], 0)
    return full.at[1:, :16].add(tails), full[-1, rows:].astype(F32)


def gather_plain(own, vectors, n):
    full, vecs = gather_whole(own, vectors, n)
    return full[:, : own.shape[0] - 16].reshape(-1, D), vecs


def pick(array, at, axis):
    return lax.dynamic_index_in_dim(array, at, axis, keepdims=False)


def total_of(terms):
    return sum(t.astype(F32) for t in terms)


def hold(value, *others):
    return lax.optimization_barrier((value, *others))[0]


def begin_plane(kept, sent):
    return [a.reshape(-1, 2, 2, *a.shape[1:]) for a in (kept, shifted(sent, "core", 1))]


def halve(terms, name, axis, aways=None):
    at = place_of(name)
    away = total_of([pick(t, 1 - at, axis) for t in terms]).astype(BF)
    if aways is not None:
        aways.append(away)
    return [pick(t, at, axis) for t in terms] + [shifted(away, name, 1)]


def first_ways(terms, aways=None):
    half = terms[0].shape[0] // 2
    return halve([t[:half] for t in terms], "x", 2, aways), halve([t[half:] for t in terms], "y", 1, aways)


def second_ways(ways):
    one, two = halve(ways[0], "y", 1), halve(ways[1], "x", 1)
    return [jnp.concatenate([a, b]) for a, b in zip(one, two)]


def send_line(planes, base, aways=None):
    count = planes[0].shape[0]
    z = place_of("z")
    sums = total_of(planes).astype(BF)
    pieces = []
    for step in (1, 2, 3):
        pairs = []
        for device in range(32):
            goal = (device // 8 + step) % 4
            if base <= goal < base + count:
                pairs.append((device, goal * 8 + device % 8))
        away = pick(sums, jnp.clip((z + step) % 4 - base, 0, count - 1), 0)
        if aways is not None:
            aways.append(away)
        pieces.append(lax.ppermute(away, "fsdp", pairs))
    return pieces


def end_line(planes, pieces, base):
    at = jnp.clip(place_of("z") - base, 0, planes[0].shape[0] - 1)
    return total_of([pick(t, at, 0) for t in planes] + pieces)


def own_part(own, vectors, local, n):
    return lax.dynamic_slice(own.reshape(-1), (vectors * D // n * lax.axis_index("fsdp"),), (local,))


def scatter_plain(matrices, vectors_sum, n):
    rows = matrices.shape[0] // n
    blocks = matrices.reshape(n, rows, D)
    tails = jnp.concatenate([blocks[1:, :16], vectors_sum[None].astype(BF)], axis=0)
    terms = jnp.concatenate([blocks, tails], axis=1).reshape(-1, D)
    return lax.psum_scatter(terms, "fsdp", scatter_dimension=0, tiled=True).astype(F32)


def on_device(src, tgt, ls, lt, enc_weights, dec_weights, cotangent, n):
    split = n == 32
    e_own, d_own = own_rows(enc_weights, 4, n), own_rows(dec_weights, 6, n)
    if split:
        b, c = at_home(e_own[:64]), at_home(e_own[64:])
        c, b = widen(c, "z"), widen(b, "y")
        b = widen(b, "z")
        w = after(at_home(d_own), *(p for p, _ in b))
        one, two = [(p[:, :64], l) for p, l in c], [(p[:, 64:], l) for p, l in c]
        one, two, w = widen(one, "x"), widen(two, "y"), widen(w, "z")
        b, one, two = widen(b, "x"), widen(one, "y"), widen(two, "x")
        b = after(b, *(p for p, _ in w))
        ready = [(0, 64, widen(b, "core")), (64, 128, widen(one, "core")), (128, 208, widen(two, "core"))]
        e_all, ev = assemble(ready, n, 192, 4, 0)
        e_all = e_all.reshape(-1, D)
        low, high = [(p[:, :144], l) for p, l in w], [(p[:, 144:], l) for p, l in w]
        low, high = widen(low, "x"), widen(high, "y")
        low, high = after(low, ev), after(high, ev)
        low, high = widen(low, "y"), widen(high, "x")
    else:
        e_all, ev = gather_plain(e_own, 4, n)
        d_all, dv = gather_plain(d_own, 6, n)
    q1, k1, v1, o1, pre1, axl, lse1, hx, gpx, sum2, enc, wup_e = forward(("full",), (ls,), src, None, e_all, ev)
    if split:
        low, high = after(low, enc), after(high, enc)
        d_all, dv = assemble([(0, 144, widen(low, "core")), (144, 272, widen(high, "core"))], n, 256, 6, 1)
    q3, k3, v3, o3, pre3, h1l, lse3, q4, k4, v4, o4, pre4, h2l, lse4, hy, gpy, sum5, final, wup_d = forward(
        ("causal", "cross"), (lt, ls), tgt, enc, d_all, dv
    )
    if split:
        d_plan = [("owned", 256, ((16, 16),)), ("owned", 256, ((8, 8),)), ("owned", 256, ((0, 8),))]
        e_plan = [("owned", 192, ((16, 16), (10, 6))), ("owned", 192, ((0, 16),))]
    else:
        d_plan = [("plain", 2 * FF, 2 * FF), ("plain", FF, FF), ("plain", 0, FF)]
        e_plan = [("plain", FF, 2 * FF), ("plain", 0, FF)]
    g3, first3, dgb, ds5, ds4 = ffn_bwd(4, 2, d_plan[0], 2 * FF, cotangent, sum5, hy, gpy, h2l, pre4, wup_d, d_all, dv)
    if split:
        p23 = begin_plane(*g3)
        aways = []
        p23 = halve(p23, "x", 2, aways)
        ds4 = hold(ds4, *aways)
    g2, first2, dgb, ds3, denc = attn_bwd(
        "cross", 0, d_plan[1], FF, lt, ls, ds4, q4, k4, v4, o4, lse4, h1l, enc, d_all, dv, pre3, dgb, first3
    )
    if split:
        p23[-1], ds3, *g2 = lax.optimization_barrier((p23[-1], ds3, *g2))
        p1 = begin_plane(*g2)
        aways = []
        p23, p1 = halve(p23, "y", 1, aways), halve(p1, "y", 1, aways)
        ds3 = hold(ds3, *aways)
    g1, _, tgt_grad = attn_bwd(
        "causal", 0, d_plan[2], 0, lt, lt, ds3, q3, k3, v3, o3, lse3, tgt, tgt, d_all, dv, ds5, dgb, first2
    )
    if split:
        p23[-1], p1[-1], denc, *g1 = lax.optimization_barrier((p23[-1], p1[-1], denc, *g1, tgt_grad))[:5]
        p0 = begin_plane(*g1)
        aways = []
        p1, p0 = halve(p1, "x", 1, aways), halve(p0, "x", 2, aways)
        denc = hold(denc, *aways)
    seal = 3 * FF if split else None
    f, first, egb, ds2, ds1 = ffn_bwd(2, 0, e_plan[0], FF, denc, sum2, hx, gpx, axl, pre1, wup_e, e_all, ev, dgb, seal=seal)
    if split:
        p1[-1], p0[-1], ds1, *f = lax.optimization_barrier((p1[-1], p0[-1], ds1, *f))
        e23 = begin_plane(*f[:2])
        p0 = halve(p0, "y", 1)
        aways = []
        e23 = first_ways(e23, aways)
        d_planes = [jnp.concatenate(t) for t in zip(p0, p1, p23)]
        dz = send_line(d_planes, 0, aways)
        ds1 = hold(ds1, *aways)
    a, _, src_grad = attn_bwd(
        "full", 0, e_plan[1], 0, ls, ls, ds1, q1, k1, v1, o1, lse1, src, src, e_all, ev, ds2, egb, first, f[2:]
    )
    if split:
        aways = []
        e01 = first_ways(begin_plane(*a), aways)
        e23[0][-1], e23[1][-1], *dz = lax.optimization_barrier((e23[0][-1], e23[1][-1], *dz, *aways))[:5]
        e_planes = [jnp.concatenate(t) for t in zip(second_ways(e01), second_ways(e23))]
        ez = send_line(e_planes, 0)
        d_sum = end_line(d_planes, dz, 0)
        e_sum = end_line(e_planes, ez, 0)
        tail = jnp.where(lax.axis_index("fsdp") == n - 1, jnp.roll(e_sum[-16:], -4, axis=0), d_sum[-16:])
        d_sum = jnp.concatenate([d_sum[:-16], tail])
    else:
        vecs = lax.psum(jnp.concatenate([egb, dgb]), "fsdp")
        d_sum = scatter_plain(jnp.concatenate([g1[0], g2[0], g3[0]]), vecs[16:], n)
        e_sum = scatter_plain(jnp.concatenate([a[0], f[0]]), vecs[:16], n)
    enc_grad = own_part(e_sum, 4, enc_weights.shape[0], n)
    dec_grad = own_part(d_sum, 6, dec_weights.shape[0], n)
    return final, src_grad, tgt_grad, enc_grad, dec_grad


def solution(mesh):
    n = mesh.shape["fsdp"]
    return jax.shard_map(
        functools.partial(on_device, n=n),
        mesh=mesh,
        in_specs=(P("fsdp", None),) * 4 + (P("fsdp"),) * 2 + (P("fsdp", None),),
        out_specs=(P("fsdp", None),) * 3 + (P("fsdp"),) * 2,
        check_vma=False,
    )
```

```python
import functools
import math

import jax
import jax.numpy as jnp
from jax import lax
from jax.experimental import pallas as pl
from jax.experimental.pallas import tpu as pltpu
from jax.sharding import PartitionSpec as P

D=512; TILE=128; SENTS=16; LOWEST=-1e30
NT=(((1,),(1,)),((),())); TN=(((0,),(0,)),((),()))
BF=jnp.bfloat16; F32=jnp.float32

def aligned(at):
    return at if isinstance(at,int) else pl.multiple_of(at,TILE)

def ends_of(ref):
    ends=[]; total=ref[0,0]
    ends.append(total)
    for j in range(1,SENTS):
        total=total+ref[0,j]; ends.append(total)
    return ends

def seg_iota(ends, shape, dim, base=0):
    place=lax.broadcasted_iota(jnp.int32, shape, dim)+base
    seg=jnp.zeros(shape,jnp.int32)
    for e in ends: seg=seg+(place>=e).astype(jnp.int32)
    return seg

def start_of(pos, ends_q, ends_k):
    at=jnp.int32(0)
    for eq,ek in zip(ends_q,ends_k): at=jnp.where(pos>=eq, ek, at)
    return at

def half_lanes(rows):
    return lax.broadcasted_iota(jnp.int32,(rows,TILE),1)<TILE//2

def two_heads(block, low):
    zero=jnp.zeros_like(block)
    return jnp.concatenate([jnp.where(low,block,zero),jnp.where(low,zero,block)],axis=0)

def window_start(kind, tile, blocks, ends_q, ends_k, width):
    if kind=="cross":
        first=start_of(tile*TILE, ends_q, ends_k)//TILE
    else:
        first=tile-1
    return pl.multiple_of(jnp.clip(first,0,blocks-width//TILE)*TILE,TILE)

WIDTH={"full":384,"causal":256,"cross":512}

VM=pl.BlockSpec(memory_space=pltpu.VMEM); SM=pl.BlockSpec(memory_space=pltpu.SMEM)
FF = 2048
EPSILON = 1e-05

def dot(a, b, dims=(((1,), (0,)), ((), ()))):
    return lax.dot_general(a, b, dims, preferred_element_type=F32)


def row_tile(i, size):
    return pl.ds(pl.multiple_of(i * size, size), size)


class Moves:
    def __init__(self, sems):
        self.sems, self.used, self.coming, self.going = sems, 0, [], []

    def copy(self, source, target):
        made = pltpu.make_async_copy(source, target, self.sems.at[self.used])
        self.used += 1
        made.start()
        return made

    def fetch(self, source, target, tile=None):
        self.coming.append((target, tile, self.copy(source, target if tile is None else target.at[rows_of(tile)])))

    def ready(self, *refs, tile=None):
        left = []
        for entry in self.coming:
            if any(entry[0] is ref for ref in refs) and (tile is None or entry[1] in (None, tile)):
                entry[2].wait()
            else:
                left.append(entry)
        self.coming = left

    def ready_all(self):
        for entry in self.coming:
            entry[2].wait()
        self.coming = []

    def send(self, source, target):
        self.going.append(self.copy(source, target))

    def finish(self):
        self.ready_all()
        for made in self.going:
            made.wait()


ROWS = 512


def rows_of(tile):
    return slice(tile * ROWS, (tile + 1) * ROWS)


def call(body, scalars, ins, outs, raw_outs, scratch, micros, raw_ins=(), alias=False, tiled=0):
    ins = [a if isinstance(a, tuple) else (a, 0, a.shape[0]) for a in ins]
    tall = [(count, *a.shape[1:]) for a, _, count in ins]
    tiles = tall[0][0] // ROWS if tiled else 1

    def kernel(*refs):
        refs = list(refs)

        def cut(count):
            taken = refs[:count]
            del refs[:count]
            return taken

        words, sources, raw_in, targets, raw = (
            cut(len(scalars)), cut(len(ins)), cut(len(raw_ins)), cut(len(outs)), cut(len(raw_outs))
        )
        in_refs, out_refs, own = cut(len(ins)), cut(len(outs)), cut(len(scratch))
        moves = Moves(refs[0])
        pairs = list(zip(sources, in_refs, ins))
        for tile in range(tiles):
            for source, target, _ in pairs[:tiled]:
                moves.fetch(source.at[rows_of(tile)], target, tile)
            if tile == 0:
                for source, target, (_, first, count) in pairs[tiled:]:
                    moves.fetch(source.at[pl.ds(first, count)], target)
        place = {id(ref): target for ref, target in zip(out_refs, targets)}

        def emit(*done, tile=None):
            for ref in done:
                if id(ref) not in place:
                    continue
                part = (lambda r: r) if tile is None else (lambda r: r.at[rows_of(tile)])
                moves.send(part(ref), part(place[id(ref)]))

        body(moves, emit, words, in_refs, raw_in, out_refs, raw, own)
        moves.finish()

    anywhere = pl.BlockSpec(memory_space=pl.ANY)
    held = [*((s, a.dtype) for s, (a, _, _) in zip(tall, ins)), *outs]
    room = sum(math.prod(s) * jnp.dtype(d).itemsize for s, d in held)
    room += sum(math.prod(s.shape) * jnp.dtype(s.dtype).itemsize for s in scratch)
    return pl.pallas_call(
        kernel,
        out_shape=tuple(jax.ShapeDtypeStruct(s, d) for s, d in (*outs, *raw_outs)),
        in_specs=[SM] * len(scalars) + [anywhere] * (len(ins) + len(raw_ins)),
        out_specs=(anywhere,) * (len(outs) + len(raw_outs)),
        scratch_shapes=[
            *(pltpu.VMEM(s, d) for s, d in held),
            *scratch,
            pltpu.SemaphoreType.DMA((len(ins) + tiled * (tiles - 1) + len(outs) * tiles + 8,)),
        ],
        input_output_aliases={len(scalars) + len(ins): len(outs)} if alias else {},
        cost_estimate=pl.CostEstimate(flops=int(micros * 1e10), bytes_accessed=2**20, transcendentals=0),
        compiler_params=pltpu.CompilerParams(vmem_limit_bytes=max(room + 8 * 2**20, 56 * 2**20)),
    )(*scalars, *(a for a, _, _ in ins), *raw_ins)


class Plain:
    def __init__(self, base, ref):
        self.base, self.ref = base, ref

    def put(self, first, value):
        if first - self.base < self.ref.shape[0]:
            self.ref[first - self.base : first - self.base + value.shape[0], :] = value


class Laid:
    def __init__(self, rows, base, ref):
        self.rows, self.base, self.ref = rows, base, ref

    def put(self, first, value):
        last = first + value.shape[0]
        for owner in range(first // self.rows, (last - 1) // self.rows + 1):
            low, high = max(first, owner * self.rows), min(last, (owner + 1) * self.rows)
            self.store(owner, low - owner * self.rows, value[low - first : high - first])
            if low == owner * self.rows:
                self.store(owner - 1, self.rows, value[low - first : low - first + 16])

    def store(self, owner, at, value):
        if 0 <= owner - self.base < self.ref.shape[0]:
            self.ref[owner - self.base, at : at + value.shape[0], :] = value


class Owned(Laid):
    def __init__(self, rows, base, kept, sent):
        self.rows, self.base, self.kept, self.sent = rows, base, kept, sent
        self.core = lax.axis_index("fsdp") % 2

    def store(self, owner, at, value):
        pair = (owner - self.base) // 2
        if not 0 <= pair < self.kept.shape[0]:
            return

        @pl.when(self.core == owner % 2)
        def _():
            self.kept[pair, at : at + value.shape[0], :] = value

        @pl.when(self.core != owner % 2)
        def _():
            self.sent[pair, at : at + value.shape[0], :] = value


def sinks_of(plan, refs):
    if plan[0] == "plain":
        return [Plain(plan[1], refs[0])]
    if plan[0] == "laid":
        return [Laid(plan[1], plan[2], refs[0])]
    return [Owned(plan[1], base, refs[2 * i], refs[2 * i + 1]) for i, (base, _) in enumerate(plan[2])]


def sink_shapes(plan):
    if plan[0] == "plain":
        return [((plan[2], D), BF)]
    if plan[0] == "laid":
        return [((plan[3], plan[1] + 16, D), BF)]
    return [((owners // 2, plan[1] + 16, D), BF) for _, owners in plan[2] for _ in range(2)]


def put_all(sinks, first, value):
    for sink in sinks:
        sink.put(first, value)


def matrix(ref, first, rows):
    if len(ref.shape) == 2:
        return ref[first : first + rows, :]
    each = ref.shape[1] - 16
    return ref[first // each : (first + rows) // each, :each, :].reshape(rows, D)


def part_of(w, first, rows):
    each = 1 if len(w.shape) == 2 else w.shape[1] - 16
    return w, first // each, rows // each


def normed(values, gain, bias):
    center = jnp.mean(values, axis=1, keepdims=True)
    shifted = values - center
    spread = jnp.mean(shifted * shifted, axis=1, keepdims=True)
    return shifted * lax.rsqrt(spread + EPSILON) * gain + bias


def norm_back(values, gain, upstream):
    center = jnp.mean(values, axis=1, keepdims=True)
    shifted = values - center
    r = lax.rsqrt(jnp.mean(shifted * shifted, axis=1, keepdims=True) + EPSILON)
    hat = shifted * r
    scaled = upstream * gain
    inner = jnp.mean(scaled * hat, axis=1, keepdims=True)
    grad = r * (scaled - jnp.mean(scaled, axis=1, keepdims=True) - hat * inner)
    return grad, jnp.sum(upstream * hat, axis=0, keepdims=True), jnp.sum(upstream, axis=0, keepdims=True)


def gelu_both(u):
    bell = jnp.exp(u * u * -0.5)
    t = 1.0 / (1.0 + jnp.abs(u) * (0.3275911 * 0.7071067811865476))
    poly = 0.5 * 1.061405429 * t - 0.5 * 1.453152027
    for c in (1.421413741, -0.284496736, 0.254829592):
        poly = poly * t + 0.5 * c
    tail = poly * t * bell
    cdf = jnp.where(u >= 0, 1.0 - tail, tail)
    return u * cdf, cdf + u * bell * 0.3989422804014327


def interleave(size):
    out = lax.broadcasted_iota(jnp.int32, (size, size), 0)
    come = lax.broadcasted_iota(jnp.int32, (size, size), 1)
    quarter = size // 4
    return jnp.where((out % quarter) * 4 + out // quarter == come, 1.0, 0.0).astype(BF)


def ffn_fwd_body(at, moves, emit, words, ins, raw_in, outs, raw, own):
    a_ref, res_ref, w_ref, vec_ref = ins
    h_ref, gp_ref, v_ref, low_ref, wup_ref = outs
    tokens = a_ref.shape[0]
    order = interleave(256)
    moves.ready(w_ref)
    for g in range(FF // 256):
        block = dot(order, matrix(w_ref, g * 256, 256)).astype(BF)
        for k in range(4):
            wup_ref[k, g * 64 : (g + 1) * 64, :] = block[k * 64 : (k + 1) * 64]
    emit(wup_ref)
    moves.ready(vec_ref)
    gain, bias = vec_ref[at : at + 1, :], vec_ref[at + 1 : at + 2, :]
    for i in range(tokens // ROWS):
        rows = rows_of(i)
        moves.ready(a_ref, res_ref, tile=i)
        a = a_ref[rows, :]
        low = a.astype(BF)
        total = a + res_ref[rows, :].astype(F32)
        for k in range(4):
            lanes = slice(k * D, (k + 1) * D)
            act, slope = gelu_both(dot(low, wup_ref[k]))
            act = act.astype(BF)
            h_ref[rows, lanes] = act
            gp_ref[rows, lanes] = slope.astype(BF)
            total = total + dot(act, matrix(w_ref, FF + k * D, D))
        v_ref[rows, :] = total
        low_ref[rows, :] = normed(total, gain, bias).astype(BF)
        emit(low_ref, v_ref, h_ref, gp_ref, tile=i)


def ffn_bwd_body(at, before, plan, base, seal, count, moves, emit, words, ins, raw_in, outs, raw, own):
    e_ref, v_ref, gp_ref, pre_ref, down_ref, wup_ref, vec_ref, h_ref, low_ref, *others = ins
    sink_refs, (first_ref, dgb_ref, ds_ref, dp_ref) = outs[:count], outs[count:]
    du_ref, dsl_ref, dk_ref = own
    sinks = sinks_of(plan, sink_refs)
    tokens = v_ref.shape[0]
    moves.ready(down_ref, wup_ref, vec_ref)
    gain, gain_pre = vec_ref[at : at + 1, :], vec_ref[before : before + 1, :]

    sums = (jnp.zeros((1, D), F32),) * 4
    for i in range(tokens // ROWS):
        rows = rows_of(i)
        moves.ready(e_ref, v_ref, gp_ref, pre_ref, tile=i)
        grad, dg, db = norm_back(v_ref[rows, :], gain, e_ref[rows, :].astype(F32))
        ds_ref[rows, :] = grad
        gl = grad.astype(BF)
        dsl_ref[rows, :] = gl
        for k in range(4):
            lanes = slice(k * D, (k + 1) * D)
            du = (dot(gl, matrix(down_ref, k * D, D), NT) * gp_ref[rows, lanes].astype(F32)).astype(BF)
            du_ref[rows, lanes] = du
            grad = grad + dot(du, wup_ref[k], NT)
        grad, dg_pre, db_pre = norm_back(pre_ref[rows, :], gain_pre, grad)
        dp_ref[rows, :] = grad
        emit(dp_ref, ds_ref, tile=i)
        sums = tuple(c + d for c, d in zip(sums, (dg_pre, db_pre, dg, db)))

    vectors = jnp.concatenate([*sums, jnp.zeros((12, D), F32)], axis=0)
    dgb_ref[...] = vectors
    if others:
        moves.ready(*others)
        vectors = jnp.concatenate([vectors[:4], others[0][:12, :]], axis=0)
    if seal is not None:
        put_all(sinks, seal, vectors.astype(BF))
    emit(dgb_ref)
    moves.ready(h_ref, low_ref)
    for k in range(8):
        piece = dot(h_ref[:, k * 256 : (k + 1) * 256], dsl_ref[...], TN).astype(BF)
        put_all(sinks, base + FF + k * 256, piece)
    for k in range(4):
        for half in range(2):
            lanes = slice(half * 256, (half + 1) * 256)
            dk_ref[k, lanes, :] = dot(low_ref[:, lanes], du_ref[:, k * D : (k + 1) * D], TN).astype(BF)
    order = interleave(256)
    for g in range(FF // 256):
        block = jnp.concatenate([dk_ref[k, g * 64 : (g + 1) * 64, :] for k in range(4)], axis=0)
        piece = dot(order, block, TN).astype(BF)
        put_all(sinks, base + g * 256, piece)
        if g == 0:
            first_ref[...] = piece[:16]
    emit(first_ref, *sink_refs)


def ffn_bwd(at, before, plan, base, e, v, h, gp, low, pre, wup, w, vecs, *others, seal=None):
    t = v.shape[0]
    shapes = sink_shapes(plan)
    outs = call(
        functools.partial(ffn_bwd_body, at, before, plan, base, seal, len(shapes)),
        (),
        (e, v, gp, pre, part_of(w, base + FF, FF), wup, vecs, h, low, *others),
        [*shapes, ((16, D), BF), ((16, D), F32), ((t, D), F32), ((t, D), F32)],
        [],
        [pltpu.VMEM((t, FF), BF), pltpu.VMEM((t, D), BF), pltpu.VMEM((4, D, D), BF)],
        13,
        tiled=4,
    )
    return outs[: len(shapes)], *outs[len(shapes) :]


def attn_fwd_body(kind, at, moves, emit, words, ins, raw_in, outs, raw, own):
    lq_ref, lk_ref = words
    xq_ref, xk_ref, w_ref, vec_ref = ins if kind == "cross" else (ins[0], *ins)
    q_ref, k_ref, v_ref, o_ref, pre_ref, out_ref, low_ref, lse_ref = outs
    (segk_ref,) = own
    tokens = q_ref.shape[0]
    blocks, width = tokens // TILE, WIDTH[kind]
    ends_q, ends_k = ends_of(lq_ref), ends_of(lk_ref)
    segk_ref[...] = seg_iota(ends_k, (8, tokens), 1)
    low = half_lanes(TILE)
    moves.ready(w_ref)
    for i in range(tokens // ROWS):
        rows = rows_of(i)
        moves.ready(xq_ref, xk_ref, tile=i)
        xq, xk = xq_ref[rows, :].astype(BF), xk_ref[rows, :].astype(BF)
        q_ref[rows, :] = dot(xq, matrix(w_ref, 0, D)).astype(BF)
        k_ref[rows, :] = dot(xk, matrix(w_ref, D, D)).astype(BF)
        v_ref[rows, :] = dot(xk, matrix(w_ref, 2 * D, D)).astype(BF)
    emit(q_ref, k_ref, v_ref)

    def one(tile, start, width, with_logs):
        rows = row_tile(tile, TILE)
        seg_q = seg_iota(ends_q, (TILE, TILE), 0, tile * TILE)
        biases = []
        for b in range(width // TILE):
            ok = seg_q == segk_ref[0:1, pl.ds(aligned(start + b * TILE), TILE)]
            if kind == "causal":
                gap = lax.broadcasted_iota(jnp.int32, (TILE, TILE), 0) - lax.broadcasted_iota(jnp.int32, (TILE, TILE), 1)
                ok = ok & (gap >= start + b * TILE - tile * TILE)
            biases.append(jnp.where(ok, 0.0, LOWEST))
        bias_q = jnp.concatenate(biases, axis=1)
        bias_q = jnp.concatenate([bias_q, bias_q], axis=0)
        outs = []
        lane = lax.broadcasted_iota(jnp.int32, (TILE, TILE), 1)
        logs = jnp.zeros((TILE, TILE), F32)
        for p in range(D // TILE):
            lanes = slice(p * TILE, (p + 1) * TILE)
            q2 = two_heads(q_ref[rows, lanes].astype(F32) * 0.125, low).astype(BF)
            s = dot(q2, k_ref[pl.ds(start, width), lanes], NT) + bias_q
            top = jnp.max(s, axis=1, keepdims=True)
            e = jnp.exp(s - top).astype(BF)
            vx = jnp.concatenate([v_ref[pl.ds(start, width), lanes], jnp.ones((width, TILE), BF)], axis=1)
            o2 = dot(e, vx)
            if with_logs:
                log = top + jnp.log(o2[:, TILE:])
                logs = jnp.where(lane == 2 * p, log[:TILE], jnp.where(lane == 2 * p + 1, log[TILE:], logs))
            o2 = o2[:, :TILE] / o2[:, TILE:]
            outs.append(jnp.where(low, o2[:TILE], o2[TILE:]))
        if with_logs:
            lse_ref[:, rows] = logs.T[:8, :]
        return jnp.concatenate(outs, axis=1)

    def step(tile, _):
        rows = row_tile(tile, TILE)
        start = window_start(kind, tile, blocks, ends_q, ends_k, width)
        o_ref[rows, :] = one(tile, start, width, True).astype(BF)
        tail = (blocks - 3) * TILE
        if kind == "cross":
            more = ends_q[-1] < (tile + 1) * TILE
        elif kind == "full":
            more = (tile == blocks - 3) & (ends_q[-1] < tail + TILE)
        else:
            more = (tile == blocks - 1) & (ends_q[-1] < tail + TILE)

        @pl.when(more)
        def _():
            o = one(tile, tail, 3 * TILE, False)
            if kind == "cross":
                mean = jnp.sum(v_ref[...].astype(F32), axis=0, keepdims=True) * (1.0 / tokens)
                o = jnp.where(ends_k[-1] >= tokens, jnp.broadcast_to(mean, o.shape), o)
            pad = lax.broadcasted_iota(jnp.int32, (TILE, D), 0) + tile * TILE >= ends_q[-1]
            o_ref[rows, :] = jnp.where(pad, o, o_ref[rows, :].astype(F32)).astype(BF)

        return 0

    lax.fori_loop(0, blocks, step, 0)
    emit(o_ref, lse_ref)
    moves.ready(vec_ref)
    gain, bias = vec_ref[at : at + 1, :], vec_ref[at + 1 : at + 2, :]

    for i in range(tokens // ROWS):
        rows = rows_of(i)
        total = xq_ref[rows, :].astype(F32) + dot(o_ref[rows, :], matrix(w_ref, 3 * D, D))
        pre_ref[rows, :] = total
        out = normed(total, gain, bias)
        out_ref[rows, :] = out
        low_ref[rows, :] = out.astype(BF)
        emit(out_ref, low_ref, pre_ref, tile=i)


def forward_body(kinds, moves, emit, words, ins, raw_in, outs, raw, own):
    *inputs, vec_ref = ins
    segk_ref, *mids = own
    at = 0
    x_ref = res_ref = inputs.pop(0)
    for i, kind in enumerate(kinds):
        lengths = (words[0], words[-1]) if kind == "cross" else (words[0], words[0])
        sources = (x_ref, inputs.pop(0)) if kind == "cross" else (x_ref,)
        low_outs = outs[7 * i : 7 * i + 7]
        attn_fwd_body(
            kind, at, moves, emit, lengths, (*sources, inputs.pop(0), vec_ref), raw_in,
            (*low_outs[:5], mids[i], *low_outs[5:]), raw, (segk_ref,)
        )
        x_ref = mids[i]
        at += 2
    ffn_fwd_body(at, moves, emit, words, (x_ref, res_ref, inputs.pop(0), vec_ref), raw_in, outs[7 * len(kinds) :], raw, ())


def forward(kinds, lengths, x, other, w, vecs):
    t = x.shape[0]
    low, full = ((t, D), BF), ((t, D), F32)
    ins = [x]
    for i, kind in enumerate(kinds):
        ins += ([other] if kind == "cross" else []) + [part_of(w, i * FF, FF)]
    return call(
        functools.partial(forward_body, kinds),
        lengths,
        (*ins, part_of(w, len(kinds) * FF, 2 * FF), vecs),
        [low, low, low, low, full, low, ((8, t), F32)] * len(kinds)
        + [((t, FF), BF), ((t, FF), BF), full, low, ((4, D, D), BF)],
        [],
        [pltpu.VMEM((8, t), jnp.int32)] + [pltpu.VMEM(*full)] * len(kinds),
        30,
    )


BACK_WIDTH = {"full": 384, "causal": 256, "cross": 272}


def four_heads(block):
    owner = lax.broadcasted_iota(jnp.int32, block.shape, 1) // 64
    return jnp.concatenate([jnp.where(owner == h, block, 0.0) for h in range(4)], axis=0).astype(BF)


def attn_bwd_body(kind, before, plan, base, seal, count, moves, emit, words, ins, raw_in, outs, raw, own):
    cross = kind == "cross"
    lq_ref, lk_ref = words
    if cross:
        ds_ref, o_ref, w_ref, lse_ref, q_ref, k_ref, v_ref, vec_ref, more_ref, xq_ref, xk_ref, dgb_in_ref, next_ref = ins
        sink_refs, (first_ref, dgb_ref, dx_ref, dxk_ref) = outs[:count], outs[count:]
    else:
        ds_ref, o_ref, w_ref, lse_ref, q_ref, k_ref, v_ref, vec_ref, more_ref, xq_ref, dgb_in_ref, next_ref = ins
        xk_ref, dxk_ref = xq_ref, None
        sink_refs, (first_ref, dx_ref) = outs[:count], outs[count:]
    segq_ref, segk_ref, inner_ref, dk_acc, dv_acc, dsl_ref, g_ref, dq_ref, dk_ref, dv_ref = own
    sinks = sinks_of(plan, sink_refs)
    for source, target in zip(raw_in, sink_refs):
        pairs = source.shape[0]
        moves.fetch(source, target.at[pl.ds(target.shape[0] - pairs, pairs)])
    tokens = q_ref.shape[0]
    blocks, width = tokens // TILE, BACK_WIDTH[kind]
    ends_q, ends_k = ends_of(lq_ref), ends_of(lk_ref)
    segq_ref[...] = seg_iota(ends_q, (8, tokens), 1)
    segk_ref[...] = seg_iota(ends_k, (tokens, TILE), 0)
    dk_acc[...] = jnp.zeros_like(dk_acc)
    dv_acc[...] = jnp.zeros_like(dv_acc)
    low = half_lanes(TILE)
    moves.ready(w_ref)
    heads = lax.broadcasted_iota(jnp.int32, (16, D), 1) // (D // 8) == lax.broadcasted_iota(jnp.int32, (16, D), 0)
    heads = jnp.where(heads, 1.0, 0.0).astype(BF)
    for i in range(tokens // ROWS):
        rows = rows_of(i)
        moves.ready(ds_ref, o_ref, tile=i)
        gl = ds_ref[rows, :].astype(BF)
        dsl_ref[rows, :] = gl
        g = dot(gl, matrix(w_ref, 3 * D, D), NT).astype(BF)
        g_ref[rows, :] = g
        both = g.astype(F32) * o_ref[rows, :].astype(F32)
        coarse = both.astype(BF)
        fine = (both - coarse.astype(F32)).astype(BF)
        inner_ref[:, rows] = dot(heads, coarse, NT) + dot(heads, fine, NT)
    moves.ready(q_ref, k_ref, v_ref, lse_ref)

    def step(tile, _):
        rows = row_tile(tile, TILE)
        start = window_start(kind, tile, blocks, ends_q, ends_k, width)
        win = pl.ds(start, width)
        ok = segk_ref[win, :] == segq_ref[0:1, rows]
        if kind == "causal":
            gap = lax.broadcasted_iota(jnp.int32, (width, TILE), 1) - lax.broadcasted_iota(jnp.int32, (width, TILE), 0)
            ok = ok & (gap >= start - tile * TILE)
        mask = jnp.where(ok, 0.0, LOWEST)
        mask = jnp.concatenate([mask, mask], axis=1)
        qs, gs = q_ref[rows, :], g_ref[rows, :]
        ks, vs = k_ref[win, :], v_ref[win, :]
        lses, inners = lse_ref[:, rows], inner_ref[:, rows]
        dks, dvs, dqs = [], [], []
        for p in range(D // TILE):
            lanes = slice(p * TILE, (p + 1) * TILE)
            q2 = two_heads(qs[:, lanes].astype(F32) * 0.125, low).astype(BF)
            g2 = two_heads(gs[:, lanes].astype(F32), low).astype(BF)
            lse = jnp.concatenate([lses[2 * p : 2 * p + 1], lses[2 * p + 1 : 2 * p + 2]], axis=1)
            inner = jnp.concatenate([inners[2 * p : 2 * p + 1], inners[2 * p + 1 : 2 * p + 2]], axis=1)
            prob = jnp.exp(dot(ks[:, lanes], q2, NT) + mask - lse)
            ds = (prob * (dot(vs[:, lanes], g2, NT) - inner)).astype(BF)
            dks.append(dot(ds, q2))
            dvs.append(dot(prob.astype(BF), g2))
            dq = dot(ds, ks[:, lanes], TN)
            dqs.append(jnp.where(low, dq[:TILE], dq[TILE:]) * 0.125)
        dk_acc[win, :] += jnp.concatenate(dks, axis=1)
        dv_acc[win, :] += jnp.concatenate(dvs, axis=1)
        dq_ref[rows, :] = jnp.concatenate(dqs, axis=1).astype(BF)
        return 0

    def fine_step(tile, _):
        rows = row_tile(tile, TILE)
        segs = segq_ref[:, rows]
        lses = jnp.where(segs == SENTS, -LOWEST, lse_ref[:, rows])
        inners = inner_ref[:8, rows]
        turned = [pltpu.roll(a, TILE // 2, 1) for a in (segs, lses, inners)]
        low = lax.broadcasted_iota(jnp.int32, (1, TILE), 1) < TILE // 2
        for half in range(2):
            at = tile * TILE + half * (TILE // 2)
            if kind == "cross":
                start = start_of(at, ends_q, ends_k) // 16 * 16
            else:
                start = at - TILE
            start = pl.multiple_of(jnp.clip(start, 0, tokens - width), 16)
            win, mine = pl.ds(start, width), pl.ds(pl.multiple_of(at, TILE // 2), TILE // 2)

            def pair(which, a, b):
                plain, other = (segs, lses, inners)[which], turned[which]
                one, two = (plain, other) if half == 0 else (other, plain)
                return jnp.where(low, one[a : a + 1], two[b : b + 1])

            ok = segk_ref[win, :] == pair(0, 0, 0)
            if kind == "causal":
                places = lax.broadcasted_iota(jnp.int32, (width, TILE), 1) % (TILE // 2)
                ok = ok & (places - lax.broadcasted_iota(jnp.int32, (width, TILE), 0) >= start - at)
            mask = jnp.where(ok, 0.0, LOWEST)
            mask = jnp.concatenate([mask, mask], axis=1)
            for group in range(2):
                lanes = slice(group * 256, (group + 1) * 256)
                q4 = four_heads(q_ref[mine, lanes].astype(F32) * 0.125)
                g4 = four_heads(g_ref[mine, lanes].astype(F32))
                lse, inner = (
                    jnp.concatenate([pair(which, 4 * group + h, 4 * group + h + 1) for h in (0, 2)], axis=1)
                    for which in (1, 2)
                )
                kp, vp = k_ref[win, lanes], v_ref[win, lanes]
                prob = jnp.exp(dot(kp, q4, NT) + mask - lse)
                ds = (prob * (dot(vp, g4, NT) - inner)).astype(BF)
                dk_acc[win, lanes] += dot(ds, q4)
                dv_acc[win, lanes] += dot(prob.astype(BF), g4)
                dq = dot(ds, kp, TN)
                owner = lax.broadcasted_iota(jnp.int32, (TILE // 2, 256), 1) // 64
                own = dq[:64]
                for h in range(1, 4):
                    own = jnp.where(owner == h, dq[64 * h : 64 * h + 64], own)
                dq_ref[mine, lanes] = (own * 0.125).astype(BF)
        return 0

    lax.fori_loop(0, blocks, fine_step if cross else step, 0, unroll=2)
    moves.ready(vec_ref, more_ref)

    sums = (jnp.zeros((1, D), F32),) * 2
    for i in range(tokens // ROWS):
        rows = rows_of(i)
        dk, dv = dk_acc[rows, :].astype(BF), dv_acc[rows, :].astype(BF)
        dk_ref[rows, :], dv_ref[rows, :] = dk, dv
        from_q = ds_ref[rows, :] + dot(dq_ref[rows, :], matrix(w_ref, 0, D), NT)
        from_k = dot(dk, matrix(w_ref, D, D), NT) + dot(dv, matrix(w_ref, 2 * D, D), NT)
        if not cross:
            dx_ref[rows, :] = more_ref[rows, :] + from_q + from_k
            emit(dx_ref, tile=i)
            continue
        dxk_ref[rows, :] = from_k
        grad, dg, db = norm_back(more_ref[rows, :], vec_ref[before : before + 1, :], from_q)
        dx_ref[rows, :] = grad
        emit(dx_ref, dxk_ref, tile=i)
        sums = sums[0] + dg, sums[1] + db
    moves.ready(dgb_in_ref)
    if cross:
        dgb_ref[...] = jnp.concatenate([*sums, dgb_in_ref[:14, :]], axis=0)
        emit(dgb_ref)
    moves.ready_all()
    for m, (left_ref, right_ref) in enumerate(((xq_ref, dq_ref), (xk_ref, dk_ref), (xk_ref, dv_ref), (o_ref, dsl_ref))):
        for half in range(2):
            piece = dot(left_ref[:, half * 256 : (half + 1) * 256], right_ref[...], TN).astype(BF)
            put_all(sinks, base + m * D + half * 256, piece)
            if m == half == 0:
                first_ref[...] = piece[:16]
    if plan[0] == "owned" and (base + 4 * D) % plan[1] == 0:
        sinks[0].store((base + 4 * D) // plan[1] - 1, plan[1], next_ref[...])
    emit(first_ref, *sink_refs)


def attn_bwd(kind, before, plan, base, lq, lk, ds, q, k, v, o, lse, xq, xk, w, vecs, more, dgb, following, taken=()):
    t = xq.shape[0]
    low, full = ((t, D), BF), ((t, D), F32)
    vm = pltpu.VMEM
    shapes = sink_shapes(plan)
    scratch = [vm((8, t), jnp.int32), vm((t, TILE), jnp.int32), vm((16, t), F32), vm(*full), vm(*full)] + [vm(*low)] * 5
    outs = call(
        functools.partial(attn_bwd_body, kind, before, plan, base, None, len(shapes)),
        (lq, lk),
        (ds, o, part_of(w, base, 4 * D), lse, q, k, v, vecs, more)
        + ((xq, xk) if kind == "cross" else (xq,))
        + (dgb, following),
        [*shapes, ((16, D), BF)] + ([((16, D), F32), full, full] if kind == "cross" else [full]),
        [],
        scratch,
        26,
        raw_ins=taken,
        tiled=2,
    )
    return outs[: len(shapes)], *outs[len(shapes) :]


SIDES = {"z": 4, "y": 2, "x": 2, "core": 2}
STRIDE = {"z": 8, "y": 4, "x": 2, "core": 1}


def place_of(name):
    return lax.axis_index("fsdp") // STRIDE[name] % SIDES[name]


def shifted(block, name, step, n=32):
    side, stride = SIDES[name], STRIDE[name]
    pairs = []
    for device in range(n):
        at = device // stride % side
        pairs.append((device, device + ((at + step) % side - at) * stride))
    return lax.ppermute(block, "fsdp", pairs)


def widen(pieces, name):
    if len(pieces) > 1 and name != "core":
        pieces = [(jnp.concatenate([p for p, _ in pieces]), sum((l for _, l in pieces), []))]
    spot = list(SIDES).index(name)
    more = []
    for held, labels in pieces:
        for step in range(1, SIDES[name]):
            moved = [tuple(v + step * (i == spot) for i, v in enumerate(label)) for label in labels]
            more.append((shifted(held, name, step), moved))
    return pieces + more


def after(pieces, *others):
    held = lax.optimization_barrier((*(p for p, _ in pieces), *others))
    return [(p, l) for p, (_, l) in zip(held, pieces)]


def at_home(own):
    return [(own[None], [(0, 0, 0, 0)])]


def assemble_body(spans, labels, rows, vectors, keep, *refs):
    *pieces, rows_ref, vecs_ref, land, tails, tails32, row_sem, tail_sem, out_sem, vec_sem = refs
    n = land.shape[0]
    me = lax.axis_index("fsdp")
    z, y, x, core = me // 8, me // 4 % 2, me // 2 % 2, me % 2
    for piece, (first, last), names in zip(pieces, spans, labels):
        for at, (dz, dy, dx, dc) in enumerate(names):
            owner = (((z + 4 - dz) % 4 * 2 + (y + dy) % 2) * 2 + (x + dx) % 2) * 2 + (core + dc) % 2
            whole = min(last, rows) - first
            if whole > 0:
                pltpu.make_async_copy(
                    piece.at[at, pl.ds(0, whole)], land.at[owner, pl.ds(first, whole)], row_sem
                ).start()
            if last > rows:
                pltpu.make_async_copy(
                    piece.at[at, pl.ds(whole, last - rows)], tails.at[owner], tail_sem
                ).start()
    pltpu.make_async_copy(land, land, row_sem).wait()
    pltpu.make_async_copy(tails, tails, tail_sem).wait()
    spill = lax.broadcasted_iota(jnp.int32, (16, D), 0) < vectors
    for owner in range(1, n):
        tail = jnp.where(spill, tails[owner - 1].astype(F32), 0.0)
        land[owner, 0:16] = (land[owner, 0:16].astype(F32) + tail).astype(BF)
    tails32[...] = tails[n - 1].astype(F32)
    target = rows_ref.at[:, pl.ds(0, rows)] if keep else rows_ref
    out = pltpu.make_async_copy(land, target, out_sem)
    vec = pltpu.make_async_copy(tails32, vecs_ref, vec_sem)
    out.start()
    vec.start()
    out.wait()
    vec.wait()


def assemble(parts, n, rows, vectors, keep):
    pieces, spans, labels = [], [], []
    for first, last, held in parts:
        for piece, names in held:
            pieces.append(piece)
            spans.append((first, last))
            labels.append(names)
    anywhere = pl.BlockSpec(memory_space=pl.ANY)
    return pl.pallas_call(
        functools.partial(assemble_body, spans, labels, rows, vectors, keep),
        out_shape=(jax.ShapeDtypeStruct((n, rows + 16 * keep, D), BF), jax.ShapeDtypeStruct((16, D), F32)),
        in_specs=[anywhere] * len(pieces),
        out_specs=(anywhere, anywhere),
        scratch_shapes=[
            pltpu.VMEM((n, rows, D), BF), pltpu.VMEM((n, 16, D), BF), pltpu.VMEM((16, D), F32)
        ] + [pltpu.SemaphoreType.DMA] * 4,
        cost_estimate=pl.CostEstimate(flops=int(8e10), bytes_accessed=2**20, transcendentals=0),
        compiler_params=pltpu.CompilerParams(vmem_limit_bytes=56 * 2**20),
    )(*pieces)


def geometry(local, n, vectors):
    rows = (local * n // D - vectors) // n
    return rows, rows + 16


def own_rows(flat, vectors, n):
    local = flat.shape[0]
    rows, block = geometry(local, n, vectors)
    extra = vectors * D // n
    room = jnp.pad(flat, (vectors * D, block * D - local))
    return lax.dynamic_slice(room, (vectors * D - extra * lax.axis_index("fsdp"),), (block * D,)).reshape(block, D)


def gather_whole(own, vectors, n):
    block = own.shape[0]
    rows = block - 16
    full = lax.all_gather(own, "fsdp", axis=0, tiled=True).reshape(n, block, D)
    spill = jnp.arange(16)[:, None] < vectors
    tails = jnp.where(spill, full[:-1, rows:], 0)
    return full.at[1:, :16].add(tails), full[-1, rows:].astype(F32)


def gather_plain(own, vectors, n):
    full, vecs = gather_whole(own, vectors, n)
    return full[:, : own.shape[0] - 16].reshape(-1, D), vecs


def pick(array, at, axis):
    return lax.dynamic_index_in_dim(array, at, axis, keepdims=False)


def total_of(terms):
    return sum(t.astype(F32) for t in terms)


def hold(value, *others):
    return lax.optimization_barrier((value, *others))[0]


def begin_plane(kept, sent):
    return [a.reshape(-1, 2, 2, *a.shape[1:]) for a in (kept, shifted(sent, "core", 1))]


def halve(terms, name, axis, aways=None):
    at = place_of(name)
    away = total_of([pick(t, 1 - at, axis) for t in terms]).astype(BF)
    if aways is not None:
        aways.append(away)
    return [pick(t, at, axis) for t in terms] + [shifted(away, name, 1)]


def first_ways(terms, aways=None):
    half = terms[0].shape[0] // 2
    return halve([t[:half] for t in terms], "x", 2, aways), halve([t[half:] for t in terms], "y", 1, aways)


def second_ways(ways):
    one, two = halve(ways[0], "y", 1), halve(ways[1], "x", 1)
    return [jnp.concatenate([a, b]) for a, b in zip(one, two)]


def send_line(planes, base, aways=None):
    count = planes[0].shape[0]
    z = place_of("z")
    sums = total_of(planes).astype(BF)
    pieces = []
    for step in (1, 2, 3):
        pairs = []
        for device in range(32):
            goal = (device // 8 + step) % 4
            if base <= goal < base + count:
                pairs.append((device, goal * 8 + device % 8))
        away = pick(sums, jnp.clip((z + step) % 4 - base, 0, count - 1), 0)
        if aways is not None:
            aways.append(away)
        pieces.append(lax.ppermute(away, "fsdp", pairs))
    return pieces


def end_line(planes, pieces, base):
    at = jnp.clip(place_of("z") - base, 0, planes[0].shape[0] - 1)
    return total_of([pick(t, at, 0) for t in planes] + pieces)


def own_part(own, vectors, local, n):
    return lax.dynamic_slice(own.reshape(-1), (vectors * D // n * lax.axis_index("fsdp"),), (local,))


def scatter_plain(matrices, vectors_sum, n):
    rows = matrices.shape[0] // n
    blocks = matrices.reshape(n, rows, D)
    tails = jnp.concatenate([blocks[1:, :16], vectors_sum[None].astype(BF)], axis=0)
    terms = jnp.concatenate([blocks, tails], axis=1).reshape(-1, D)
    return lax.psum_scatter(terms, "fsdp", scatter_dimension=0, tiled=True).astype(F32)


def on_device(src, tgt, ls, lt, enc_weights, dec_weights, cotangent, n):
    split = n == 32
    e_own, d_own = own_rows(enc_weights, 4, n), own_rows(dec_weights, 6, n)
    if split:
        b, c = at_home(e_own[:64]), at_home(e_own[64:])
        c, b = widen(c, "z"), widen(b, "y")
        b = widen(b, "z")
        w = after(at_home(d_own), *(p for p, _ in b))
        one, two = [(p[:, :64], l) for p, l in c], [(p[:, 64:], l) for p, l in c]
        one, two, w = widen(one, "x"), widen(two, "y"), widen(w, "z")
        b, one, two = widen(b, "x"), widen(one, "y"), widen(two, "x")
        b = after(b, *(p for p, _ in w))
        ready = [(0, 64, widen(b, "core")), (64, 128, widen(one, "core")), (128, 208, widen(two, "core"))]
        e_all, ev = assemble(ready, n, 192, 4, 0)
        e_all = e_all.reshape(-1, D)
        low, high = [(p[:, :144], l) for p, l in w], [(p[:, 144:], l) for p, l in w]
        low, high = widen(low, "x"), widen(high, "y")
        low, high = after(low, ev), after(high, ev)
        low, high = widen(low, "y"), widen(high, "x")
    else:
        e_all, ev = gather_plain(e_own, 4, n)
        d_all, dv = gather_plain(d_own, 6, n)
    q1, k1, v1, o1, pre1, axl, lse1, hx, gpx, sum2, enc, wup_e = forward(("full",), (ls,), src, None, e_all, ev)
    if split:
        low, high = after(low, enc), after(high, enc)
        d_all, dv = assemble([(0, 144, widen(low, "core")), (144, 272, widen(high, "core"))], n, 256, 6, 1)
    q3, k3, v3, o3, pre3, h1l, lse3, q4, k4, v4, o4, pre4, h2l, lse4, hy, gpy, sum5, final, wup_d = forward(
        ("causal", "cross"), (lt, ls), tgt, enc, d_all, dv
    )
    if split:
        d_plan = [("owned", 256, ((16, 16),)), ("owned", 256, ((8, 8),)), ("owned", 256, ((0, 8),))]
        e_plan = [("owned", 192, ((16, 16), (10, 6))), ("owned", 192, ((0, 16),))]
    else:
        d_plan = [("plain", 2 * FF, 2 * FF), ("plain", FF, FF), ("plain", 0, FF)]
        e_plan = [("plain", FF, 2 * FF), ("plain", 0, FF)]
    g3, first3, dgb, ds5, ds4 = ffn_bwd(4, 2, d_plan[0], 2 * FF, cotangent, sum5, hy, gpy, h2l, pre4, wup_d, d_all, dv)
    if split:
        p23 = begin_plane(*g3)
        aways = []
        p23 = halve(p23, "x", 2, aways)
        ds4 = hold(ds4, *aways)
    g2, first2, dgb, ds3, denc = attn_bwd(
        "cross", 0, d_plan[1], FF, lt, ls, ds4, q4, k4, v4, o4, lse4, h1l, enc, d_all, dv, pre3, dgb, first3
    )
    if split:
        p23[-1], ds3, *g2 = lax.optimization_barrier((p23[-1], ds3, *g2))
        p1 = begin_plane(*g2)
        aways = []
        p23, p1 = halve(p23, "y", 1, aways), halve(p1, "y", 1, aways)
        ds3 = hold(ds3, *aways)
    g1, _, tgt_grad = attn_bwd(
        "causal", 0, d_plan[2], 0, lt, lt, ds3, q3, k3, v3, o3, lse3, tgt, tgt, d_all, dv, ds5, dgb, first2
    )
    if split:
        p23[-1], p1[-1], denc, *g1 = lax.optimization_barrier((p23[-1], p1[-1], denc, *g1, tgt_grad))[:5]
        p0 = begin_plane(*g1)
        aways = []
        p1, p0 = halve(p1, "x", 1, aways), halve(p0, "x", 2, aways)
        denc = hold(denc, *aways)
    seal = 3 * FF if split else None
    f, first, egb, ds2, ds1 = ffn_bwd(2, 0, e_plan[0], FF, denc, sum2, hx, gpx, axl, pre1, wup_e, e_all, ev, dgb, seal=seal)
    if split:
        p1[-1], p0[-1], ds1, *f = lax.optimization_barrier((p1[-1], p0[-1], ds1, *f))
        e23 = begin_plane(*f[:2])
        p0 = halve(p0, "y", 1)
        aways = []
        e23 = first_ways(e23, aways)
        d_planes = [jnp.concatenate(t) for t in zip(p0, p1, p23)]
        dz = send_line(d_planes, 0, aways)
        ds1 = hold(ds1, *aways)
    a, _, src_grad = attn_bwd(
        "full", 0, e_plan[1], 0, ls, ls, ds1, q1, k1, v1, o1, lse1, src, src, e_all, ev, ds2, egb, first, f[2:]
    )
    if split:
        aways = []
        e01 = first_ways(begin_plane(*a), aways)
        e23[0][-1], e23[1][-1], *dz = lax.optimization_barrier((e23[0][-1], e23[1][-1], *dz, *aways))[:5]
        e_planes = [jnp.concatenate(t) for t in zip(second_ways(e01), second_ways(e23))]
        ez = send_line(e_planes, 0)
        d_sum = end_line(d_planes, dz, 0)
        e_sum = end_line(e_planes, ez, 0)
        tail = jnp.where(lax.axis_index("fsdp") == n - 1, jnp.roll(e_sum[-16:], -4, axis=0), d_sum[-16:])
        d_sum = jnp.concatenate([d_sum[:-16], tail])
    else:
        vecs = lax.psum(jnp.concatenate([egb, dgb]), "fsdp")
        d_sum = scatter_plain(jnp.concatenate([g1[0], g2[0], g3[0]]), vecs[16:], n)
        e_sum = scatter_plain(jnp.concatenate([a[0], f[0]]), vecs[:16], n)
    enc_grad = own_part(e_sum, 4, enc_weights.shape[0], n)
    dec_grad = own_part(d_sum, 6, dec_weights.shape[0], n)
    return final, src_grad, tgt_grad, enc_grad, dec_grad


def solution(mesh):
    n = mesh.shape["fsdp"]
    return jax.shard_map(
        functools.partial(on_device, n=n),
        mesh=mesh,
        in_specs=(P("fsdp", None),) * 4 + (P("fsdp"),) * 2 + (P("fsdp", None),),
        out_specs=(P("fsdp", None),) * 3 + (P("fsdp"),) * 2,
        check_vma=False,
    )
```
